512 devices in a mesh: slab: 16 (over z_lo, y), rcv: 32 (over x, z_hi, core).
Axes of the slice: x: 4, y: 4, z: 16 (z_hi: 4, z_lo: 4; z = z_hi * 4 + z_lo), core: 2. Of those that a mesh axis runs over, the one named last changes fastest.
Arguments:
- adjoint_now: float32 [32, 64, 128, 128], P('rcv', 'slab'), may hold values from -6 to 6
- adjoint_before: float32 [32, 64, 128, 128], P('rcv', 'slab'), may hold values from -6 to 6
- courant_field: float32 [64, 128, 128], P('slab'), may hold values from 0.04 to 0.2
- log_buoyancy: float32 [64, 128, 128], P('slab'), may hold values from -0.3 to 0.3
- snapshot_store: float32 [32, 64, 128, 128], P('rcv', 'slab'), may hold values from -6 to 6
- owner_order: int32 [32], replicated, may hold values from 0 to 31, each once
- receiver_cells: int32 [32], P('rcv'), may hold values from 0 to 1048575
- receiver_traces: float32 [32, 8], P('rcv'), may hold values from -6 to 6
- residual_weights: float32 [32], P('rcv'), may hold values from -0.3 to 0.3
Outputs:
- sensitivity: float32 [64, 128, 128], P('slab', 'rcv')
- adjoint_after: float32 [32, 64, 128, 128], P('rcv', 'slab')
The draws below stay inside these ranges and needn't reach their ends.
Inputs may be any that keep to these rules, and one draw needn't show every extreme that they name: Each slot number appears once; checkpoint k reads slot owner_order[k] for k < 4. `receiver_cells`: a cell of the grid.
All inputs are finite; a program needn't handle non-finite values.
Results may differ from the reference program's by a relative error of at most 0.0003.
Values sent between devices are 32-bit elements; how exact they have to be, the bound alone decides.
A program may use at most 64 MiB of HBM per device.

```python
import math
import jax
import jax.numpy as jnp
from jax import lax

NY = 128
NZ = 128
SNAPS = 4
NX = 64
RCVS = 32
SLOTS = 32
STEPS = 8


def place_ends(entries, key, smallest, largest):
    longest = entries.shape.index(max(entries.shape))
    spots = []
    for shift in (0, 1):
        where = [jax.random.randint(jax.random.fold_in(key, axis), (), 0, length) for axis, length in enumerate(entries.shape)]
        where[longest] = (where[longest] + shift) % entries.shape[longest]
        spots.append(tuple(where))
    return entries.at[spots[0]].set(smallest).at[spots[1]].set(largest)


def block_levels(own_key, shape, cuts, smallest, largest):
    def one(position, shards_of):
        heights = jax.random.uniform(jax.random.fold_in(jax.random.fold_in(own_key, 6), position), (shards_of,), jnp.float32, smallest / len(cuts), largest / len(cuts))
        return jnp.repeat(jnp.exp(heights), shape[position] // shards_of).reshape((-1,) + (1,) * (len(shape) - position - 1))

    gain = one(*cuts[0])
    for cut in cuts[1:]:
        gain = gain * one(*cut)
    return gain


def normal_values(stream_key, dims, scale, most, cuts=(), held_as=jnp.bfloat16):
    entries = scale * jax.random.normal(stream_key, dims, jnp.float32)
    if cuts:
        entries = entries * block_levels(stream_key, dims, cuts, -0.22, 0.18)
    return jnp.clip(entries, -most, most).astype(held_as)


def setup_inputs(seed: int = 0) -> dict:
    key_list = jax.random.split(jax.random.key(seed), 10)
    adjoint_now = normal_values(key_list[0], (RCVS, NX, NY, NZ), 1.0, 6.0, ((0, 32), (1, 16)), jnp.float32)
    adjoint_before = normal_values(key_list[1], (RCVS, NX, NY, NZ), 1.0, 6.0, ((0, 32), (1, 16)), jnp.float32)
    courant_field = jnp.clip(jnp.exp(math.log(0.2) - 1.609438 * jax.random.uniform(key_list[2], (NX, NY, NZ), jnp.float32) ** block_levels(key_list[2], (NX, NY, NZ), ((0, 16),), -0.2, 0.2)), 0.04, 0.2)
    log_buoyancy = jnp.clip(jax.random.uniform(key_list[3], (NX, NY, NZ), jnp.float32, -0.3, 0.3) * block_levels(key_list[3], (NX, NY, NZ), ((0, 16),), -0.4, 0.0), -0.3, 0.3)
    snapshot_store = normal_values(key_list[4], (SLOTS, NX, NY, NZ), 1.0, 6.0, ((0, 32), (1, 16)), jnp.float32)
    owner_order = jax.random.permutation(key_list[5], SLOTS).astype(jnp.int32)
    receiver_cells = place_ends(jax.random.randint(key_list[6], (RCVS,), 0, NX * NY * NZ), jax.random.fold_in(key_list[6], 1), 0, (NX * NY * NZ) - 1).astype(jnp.int32)
    receiver_traces = normal_values(key_list[7], (RCVS, STEPS), 1.0, 6.0, ((0, 32),), jnp.float32)
    residual_weights = normal_values(key_list[8], (RCVS,), 0.05, 0.3, ((0, 32),), jnp.float32)
    return dict(adjoint_now=adjoint_now, adjoint_before=adjoint_before, courant_field=courant_field, log_buoyancy=log_buoyancy, snapshot_store=snapshot_store, owner_order=owner_order, receiver_cells=receiver_cells, receiver_traces=receiver_traces, residual_weights=residual_weights)


def piece_of(field, axis_no, begin, extent):
    return lax.slice_in_dim(field, begin, begin + extent, axis=axis_no)


def pad_axis(field, axis_no):
    widths = [(0, 0)] * field.ndim
    widths[axis_no] = (2, 2)
    return jnp.pad(field, widths)


def second_diff(field, axis_no, extent):
    outer = piece_of(field, axis_no, 0, extent) + piece_of(field, axis_no, 4, extent)
    inner = piece_of(field, axis_no, 1, extent) + piece_of(field, axis_no, 3, extent)
    return (16.0 * inner - outer - 30.0 * piece_of(field, axis_no, 2, extent)) / 12.0


def first_diff(field, axis_no, extent):
    inner = piece_of(field, axis_no, 3, extent) - piece_of(field, axis_no, 1, extent)
    outer = piece_of(field, axis_no, 4, extent) - piece_of(field, axis_no, 0, extent)
    return (8.0 * inner - outer) / 12.0


def slopes(log_ext):
    width = log_ext.shape[0] - 4
    centre = piece_of(log_ext, 0, 2, width)
    wide_y = pad_axis(centre, 1)
    wide_z = pad_axis(centre, 2)
    return jnp.stack([first_diff(log_ext, 0, width), first_diff(wide_y, 1, centre.shape[1]), first_diff(wide_z, 2, centre.shape[2])])


def advance(field, before, courant, gradient):
    first_axis = field.ndim - 3
    width = field.shape[first_axis] - 4
    centre = piece_of(field, first_axis, 2, width)
    wide_y = pad_axis(centre, first_axis + 1)
    wide_z = pad_axis(centre, first_axis + 2)
    size_y = field.shape[first_axis + 1]
    size_z = field.shape[first_axis + 2]
    curvature = second_diff(field, first_axis, width) + second_diff(wide_y, first_axis + 1, size_y) + second_diff(wide_z, first_axis + 2, size_z)
    drift_term = gradient[0] * first_diff(field, first_axis, width) + gradient[1] * first_diff(wide_y, first_axis + 1, size_y) + gradient[2] * first_diff(wide_z, first_axis + 2, size_z)
    return 2.0 * centre - before + courant * (curvature + drift_term)


def reference(adjoint_now, adjoint_before, courant_field, log_buoyancy, snapshot_store, owner_order, receiver_cells, receiver_traces, residual_weights):
    gradient = slopes(pad_axis(log_buoyancy, 0))
    snapshots = jnp.take(snapshot_store, owner_order[:SNAPS], axis=0)
    flat_ids = jnp.arange(NX * NY * NZ, dtype=jnp.int32).reshape(NX, NY, NZ)

    def receiver(kernel, item):
        current, previous, trace_row, cell_id, weight = item
        struck = flat_ids == cell_id
        for snap_index in range(SNAPS):
            for half_step in range(2):
                tick = 2 * snap_index + half_step
                upcoming = advance(pad_axis(current, 0), previous, courant_field, gradient)
                upcoming = upcoming + jnp.where(struck, trace_row[tick], 0.0)
                previous, current = current, upcoming
            kernel = kernel + (weight * current) * snapshots[snap_index]
        return kernel, current

    start_kernel = jnp.zeros((NX, NY, NZ), jnp.float32)
    sensitivity, adjoint_after = lax.scan(receiver, start_kernel, (adjoint_now, adjoint_before, receiver_traces, receiver_cells, residual_weights))
    return sensitivity, adjoint_after
```

```python
import functools

import jax
import jax.numpy as jnp
from jax import lax
from jax.experimental import pallas as pl
from jax.experimental.pallas import tpu as pltpu
from jax.sharding import PartitionSpec as P

MESH = pl.DeviceIdType.MESH
F32 = jnp.float32
SNAPS = 4
STEPS = 8
CORES = 2
ZHI = 4
ROWS = 4
CHUNKS = 4
PAD = 8
A, B, M = 0, 1, 2


def when(condition, action):
    pl.when(condition)(action)


def kernel(
    dims,
    now_ref,
    before_ref,
    courant_ref,
    log_ref,
    store_ref,
    owner_ref,
    cell_ref,
    trace_ref,
    weight_ref,
    sens_ref,
    after_ref,
    field,
    log_buf,
    courant,
    grad,
    weighted,
    group_in,
    tile_out,
    tile_in,
    snap_in,
    snap_out,
    snap_tile,
    load_sem,
    model_send,
    model_recv,
    halo_send,
    halo_recv,
    group_send,
    group_recv,
    tile_send,
    tile_recv,
    snap_send,
    snap_recv,
    stile_send,
    stile_recv,
    out_sem,
):
    slabs, xs, ny, nz = dims
    group = xs * CORES
    block = ny // group
    pairs = ZHI // CORES
    chunk = ny // CHUNKS
    s = lax.axis_index("slab")
    r = lax.axis_index("rcv")
    core = lax.rem(r, CORES)
    zh = lax.rem(r // CORES, ZHI)
    xpos = r // (CORES * ZHI)
    member = xpos * CORES + core
    has_left, has_right = s > 0, s < slabs - 1

    def rcv_of(x, z, c):
        return (x * ZHI + z) * CORES + c

    def peer(d):
        other = lax.rem(member + d, group)
        return rcv_of(other // CORES, zh, lax.rem(other, CORES))

    barrier = pltpu.get_barrier_semaphore()

    def greet(slab, rcv):
        pl.semaphore_signal(barrier, 1, device_id=(slab, rcv), device_id_type=MESH)

    when(has_left, lambda: greet(s - 1, r))
    when(has_right, lambda: greet(s + 1, r))
    for d in range(1, group):
        greet(s, peer(d))
    half = zh // pairs
    for z in range(ZHI):
        when((z != zh) | (half != core), lambda: greet(s, rcv_of(xpos, z, half)))

    own = pl.ds(ROWS, ROWS)
    ycells = pl.ds(PAD, ny)
    loads = [
        pltpu.make_async_copy(log_ref, log_buf.at[own, ycells], load_sem.at[0]),
        pltpu.make_async_copy(courant_ref, courant.at[own], load_sem.at[1]),
        pltpu.make_async_copy(now_ref.at[0], field.at[A, own, ycells], load_sem.at[2]),
        pltpu.make_async_copy(before_ref.at[0], field.at[M, own, ycells], load_sem.at[3]),
        pltpu.make_async_copy(
            store_ref.at[0, :, pl.ds(pl.multiple_of(member * block, 8), block)],
            snap_in.at[group - 1],
            load_sem.at[4],
        ),
    ]
    for load in loads:
        load.start()

    zero_pad = jnp.zeros((3 * ROWS, PAD, nz), F32)
    for slot in (A, B, M):
        field[slot, :, 0:PAD, :] = zero_pad
        field[slot, :, PAD + ny : 2 * PAD + ny, :] = zero_pad
    log_buf[:, 0:PAD, :] = zero_pad
    log_buf[:, PAD + ny : 2 * PAD + ny, :] = zero_pad

    def clear(lo):
        def body(i, carry):
            rows = pl.ds(pl.multiple_of(i * 8, 8), 8)
            shifted = pl.ds(pl.multiple_of(i * 8 + PAD, 8), 8)
            zeros = jnp.zeros((8, nz), F32)
            for row in range(lo, lo + ROWS):
                for slot in (A, B, M):
                    field[slot, row, shifted, :] = zeros
                log_buf[row, shifted, :] = zeros
                courant[row, rows, :] = zeros
            return carry

        lax.fori_loop(0, ny // 8, body, 0)

    when(jnp.logical_not(has_left), lambda: clear(0))
    when(jnp.logical_not(has_right), lambda: clear(2 * ROWS))

    mine = (zh // pairs == core).astype(jnp.int32)
    neighbours = has_left.astype(jnp.int32) + has_right.astype(jnp.int32)
    pl.semaphore_wait(barrier, neighbours + (group - 1) + ZHI - mine)

    def side_copy(side, src, dst, send, recv):
        return pltpu.make_async_remote_copy(
            src_ref=src,
            dst_ref=dst,
            send_sem=send,
            recv_sem=recv,
            device_id=(s + 1 if side == 0 else s - 1, r),
            device_id_type=MESH,
        )

    leaves = (has_right, has_left)
    comes = (has_left, has_right)

    def model_copy(which, side):
        near = (2, 0)[side]
        far = (0, 2)[side]
        land_near = (2, 8)[side]
        land_far = (0, 10)[side]
        if which == 2:
            src, dst = courant_ref.at[near : near + 2], courant.at[land_near : land_near + 2]
        else:
            at, to = ((near, land_near), (far, land_far))[which]
            src, dst = log_ref.at[at : at + 2], log_buf.at[to : to + 2, ycells]
        return side_copy(side, src, dst, model_send.at[which, side], model_recv.at[which, side])

    def halo_copy(e, side, j, deep, slot, from_input=False):
        if deep == ROWS:
            at, to = 0, (0, 2 * ROWS)[side]
        else:
            at, to = (ROWS - deep, 0)[side], (ROWS - deep, 2 * ROWS)[side]
        here = pl.ds(pl.multiple_of(j * chunk, 8), chunk)
        there = pl.ds(pl.multiple_of(j * chunk + PAD, 8), chunk)
        if from_input:
            src = now_ref.at[0, at : at + deep, here]
        else:
            src = field.at[slot, ROWS + at : ROWS + at + deep, there]
        dst = field.at[slot, to : to + deep, there]
        return side_copy(side, src, dst, halo_send.at[e, side, j], halo_recv.at[e, side, j])

    def halo_start(e, j, deep, slot, from_input=False):
        for side in (0, 1):
            copy = halo_copy(e, side, j, deep, slot, from_input)
            when(leaves[side], copy.start)

    def halo_arrive(e, j, deep, slot):
        for side in (0, 1):
            copy = halo_copy(e, side, j, deep, slot)
            when(comes[side], copy.wait_recv)

    def halo_sent(e, deep, slot, from_input=False):
        def body(j, carry):
            for side in (0, 1):
                copy = halo_copy(e, side, j, deep, slot, from_input)
                when(leaves[side], copy.wait_send)
            return carry

        lax.fori_loop(0, CHUNKS, body, 0)

    for side in (0, 1):
        when(leaves[side], model_copy(0, side).start)
    for j in range(CHUNKS):
        halo_start(0, j, 2, A, True)
    for which in (1, 2):
        for side in (0, 1):
            when(leaves[side], model_copy(which, side).start)

    def snap_copy(d):
        other = lax.rem(member + d, group)
        return pltpu.make_async_remote_copy(
            src_ref=store_ref.at[0, :, pl.ds(pl.multiple_of(other * block, 8), block)],
            dst_ref=snap_in.at[d - 1],
            send_sem=snap_send.at[d - 1],
            recv_sem=snap_recv.at[d - 1],
            device_id=(s, peer(d)),
            device_id_type=MESH,
        )

    for d in range(1, group):
        snap_copy(d).start()

    lane = lax.broadcasted_iota(jnp.int32, (8, nz), 1)
    ids = lax.broadcasted_iota(jnp.int32, (8, nz), 0) * nz + lane
    low1, low2 = lane >= 1, lane >= 2
    high1, high2 = lane < nz - 1, lane < nz - 2

    def z_shifts(u):
        zero = jnp.zeros_like(u)
        return (
            jnp.where(low2, pltpu.roll(u, 2, 1), zero),
            jnp.where(low1, pltpu.roll(u, 1, 1), zero),
            jnp.where(high1, pltpu.roll(u, nz - 1, 1), zero),
            jnp.where(high2, pltpu.roll(u, nz - 2, 1), zero),
        )

    twelfth = 1.0 / 12.0

    def slopes(rows):
        def body(i, carry):
            at = pl.ds(pl.multiple_of(i * 8, 8), 8)
            y0 = i * 8 + PAD
            mid = {}
            for row in rows:
                for k in (-2, -1, 0, 1, 2):
                    if row + k not in mid:
                        mid[row + k] = log_buf[row + k, pl.ds(pl.multiple_of(y0, 8), 8), :]
            for row in rows:
                y = [log_buf[row, pl.ds(y0 + k, 8), :] for k in (-2, -1, 1, 2)]
                z = z_shifts(mid[row])
                x = [mid[row + k] for k in (-2, -1, 1, 2)]
                for axis, u in enumerate((x, y, z)):
                    grad[axis, row, at, :] = (8.0 * (u[2] - u[1]) - (u[3] - u[0])) * twelfth
                courant[row, at, :] = courant[row, at, :] * twelfth
            return carry

        lax.fori_loop(0, ny // 8, body, 0)

    cell = cell_ref[0]
    weight = weight_ref[0]

    def advance(dst, src, prev, rows, i, amplitude, snap=None):
        at = pl.ds(pl.multiple_of(i * 8, 8), 8)
        y0 = i * 8 + PAD
        centre = pl.ds(pl.multiple_of(y0, 8), 8)
        mid = {row: field[src, row, centre, :] for row in range(rows[0] - 2, rows[-1] + 3)}
        for row in rows:
            u = mid[row]
            y = [field[src, row, pl.ds(y0 + k, 8), :] for k in (-2, -1, 1, 2)]
            z = z_shifts(u)
            x = [mid[row + k] for k in (-2, -1, 1, 2)]
            near = (x[1] + x[2]) + (y[1] + y[2]) + (z[1] + z[2])
            far = (x[0] + x[3]) + (y[0] + y[3]) + (z[0] + z[3])
            drift = [
                grad[axis, row, at, :] * (8.0 * (v[2] - v[1]) - (v[3] - v[0]))
                for axis, v in enumerate((x, y, z))
            ]
            change = (16.0 * near - far - 90.0 * u) + (drift[0] + drift[1] + drift[2])
            new = (2.0 * u - field[prev, row, centre, :]) + courant[row, at, :] * change
            base = ((s * ROWS + (row - ROWS)) * ny + i * 8) * nz
            new = new + jnp.where(ids == cell - base, amplitude, 0.0)
            field[dst, row, centre, :] = new
            if snap is not None:
                weighted[snap, row - ROWS, at, :] = weight * new

    own_rows = range(ROWS, 2 * ROWS)
    wide_rows = range(ROWS - 2, 2 * ROWS + 2)
    per = chunk // 8

    def group_copy(k, other):
        d = lax.rem(other - member + group, group)
        return d, pltpu.make_async_remote_copy(
            src_ref=weighted.at[k, :, pl.ds(pl.multiple_of(other * block, 8), block)],
            dst_ref=group_in.at[k, jnp.maximum(d - 1, 0)],
            send_sem=group_send.at[k, jnp.maximum(d - 1, 0)],
            recv_sem=group_recv.at[k, jnp.maximum(d - 1, 0)],
            device_id=(s, rcv_of(other // CORES, zh, lax.rem(other, CORES))),
            device_id_type=MESH,
        )

    def group_start(k, j):
        for other in range(group // CHUNKS):
            d, copy = group_copy(k, j * (group // CHUNKS) + other)
            when(d > 0, copy.start)

    def group_wait(k, arrival):
        for d in range(1, group):
            copy = group_copy(k, lax.rem(member + d, group))[1]
            if arrival:
                copy.wait_recv()
            else:
                copy.wait_send()

    def tile_copies(out, landing, send, recv):
        for i in range(pairs):
            for c in range(CORES):
                z = core * pairs + i
                copy = pltpu.make_async_remote_copy(
                    src_ref=out.at[i, c],
                    dst_ref=landing.at[zh],
                    send_sem=send.at[i, c],
                    recv_sem=recv.at[zh],
                    device_id=(s, rcv_of(xpos, z, c)),
                    device_id_type=MESH,
                )
                yield i, c, (z == zh) & (c == core), copy

    def tile_arrive(landing, recv):
        for z in range(ZHI):
            copy = pltpu.make_async_remote_copy(
                src_ref=landing.at[z],
                dst_ref=landing.at[z],
                send_sem=recv.at[z],
                recv_sem=recv.at[z],
                device_id=(s, rcv_of(xpos, z, half)),
                device_id_type=MESH,
            )
            when((z != zh) | (half != core), copy.wait_recv)

    def tile_start(k):
        group_wait(k, True)
        out, landing = tile_out.at[k], tile_in.at[k]
        for i, c, self_target, copy in tile_copies(out, landing, tile_send.at[k], tile_recv.at[k]):
            at = (2 * i + c) * 4
            for row in range(ROWS):
                total = weighted[k, row, pl.ds(member * block + at, 4), :]
                for d in range(group - 1):
                    total = total + group_in[k, d, row, at : at + 4, :]
                out[i, c, row] = total

            @pl.when(self_target)
            def _():
                landing[zh] = out[i, c]

            when(jnp.logical_not(self_target), copy.start)

    def tile_sent(out, landing, send, recv):
        for i, c, self_target, copy in tile_copies(out, landing, send, recv):
            when(jnp.logical_not(self_target), copy.wait_send)

    def snap_tile_start():
        loads[4].wait()
        for d in range(1, group):
            snap_copy(d).wait_recv()
        for i, c, self_target, copy in tile_copies(snap_out, snap_tile, stile_send, stile_recv):
            at = (2 * i + c) * 4
            for k in range(SNAPS):
                slot = owner_ref[k]
                holder = (slot // (CORES * ZHI)) * CORES + lax.rem(slot, CORES)
                place = lax.rem(member - holder + 2 * group - 1, group)
                for row in range(ROWS):
                    snap_out[i, c, k, row] = snap_in[place, row, at : at + 4, :]

            @pl.when(self_target)
            def _():
                snap_tile[zh] = snap_out[i, c]

            when(jnp.logical_not(self_target), copy.start)

    loads[0].wait()
    loads[1].wait()
    for side in (0, 1):
        when(comes[side], model_copy(0, side).wait_recv)
    slopes(own_rows)
    loads[2].wait()
    loads[3].wait()

    def first(j, carry):
        halo_arrive(0, j, 2, A)

        def body(i, inner):
            advance(M, A, M, own_rows, i, trace_ref[0, 0])
            return inner

        lax.fori_loop(j * per, (j + 1) * per, body, 0)
        halo_start(1, j, 2, M)
        return carry

    lax.fori_loop(0, CHUNKS, first, 0)
    for which in (1, 2):
        for side in (0, 1):
            when(comes[side], model_copy(which, side).wait_recv)
    slopes((2, 3, 8, 9))

    def second(j, carry):
        halo_arrive(1, j, 2, M)

        def body(i, inner):
            advance(B, M, A, own_rows, i, trace_ref[0, 1], 0)
            return inner

        lax.fori_loop(j * per, (j + 1) * per, body, 0)
        halo_start(2, j, ROWS, B)
        group_start(0, j)
        return carry

    lax.fori_loop(0, CHUNKS, second, 0)
    snap_tile_start()
    halo_sent(0, 2, A, True)
    halo_sent(1, 2, M)

    def pair(p, carry):
        src = lax.rem(p, 2)
        dst = 1 - src

        @pl.when(p > 1)
        def _():
            halo_sent(p, ROWS, dst)

        def part(j, inner):
            @pl.when(j == 0)
            def _():
                halo_arrive(p + 1, 0, ROWS, src)

            @pl.when(j < CHUNKS - 1)
            def _():
                halo_arrive(p + 1, j + 1, ROWS, src)

            def middle(i, deep):
                advance(M, src, M, wide_rows, i, trace_ref[0, 2 * p])
                return deep

            lax.fori_loop(
                jnp.where(j == 0, 0, j * per + 1),
                jnp.minimum((j + 1) * per + 1, ny // 8),
                middle,
                0,
            )

            def final(i, deep):
                advance(dst, M, src, own_rows, i, trace_ref[0, 2 * p + 1], p)
                return deep

            lax.fori_loop(j * per, (j + 1) * per, final, 0)
            when(p < SNAPS - 1, lambda: halo_start(p + 2, j, ROWS, dst))
            group_start(p, j)

            @pl.when(p == SNAPS - 1)
            def _():
                at = pl.ds(pl.multiple_of(j * chunk, 8), chunk)
                there = pl.ds(pl.multiple_of(j * chunk + PAD, 8), chunk)
                pltpu.make_async_copy(
                    field.at[dst, own, there], after_ref.at[0, :, at], out_sem.at[j]
                ).start()

            return inner

        lax.fori_loop(0, CHUNKS, part, 0)
        tile_start(p - 1)
        return carry

    lax.fori_loop(1, SNAPS, pair, 0)
    tile_start(SNAPS - 1)

    halo_sent(SNAPS, ROWS, B)
    for which in range(3):
        for side in (0, 1):
            when(leaves[side], model_copy(which, side).wait_send)
    for d in range(1, group):
        snap_copy(d).wait_send()
    for k in range(SNAPS):
        group_wait(k, False)
        tile_sent(tile_out.at[k], tile_in.at[k], tile_send.at[k], tile_recv.at[k])
    tile_sent(snap_out, snap_tile, stile_send, stile_recv)
    for j in range(CHUNKS):
        at = pl.ds(j * chunk, chunk)
        there = pl.ds(j * chunk + PAD, chunk)
        pltpu.make_async_copy(field.at[A, own, there], after_ref.at[0, :, at], out_sem.at[j]).wait()

    tile_arrive(snap_tile, stile_recv)
    for k in range(SNAPS):
        tile_arrive(tile_in.at[k], tile_recv.at[k])
    result = jnp.zeros((ROWS, 4, nz), F32)
    for k in range(SNAPS):
        total = (tile_in[k, 0] + tile_in[k, 1]) + (tile_in[k, 2] + tile_in[k, 3])
        holder = lax.rem(owner_ref[k] // CORES, ZHI)
        result = result + total * snap_tile[holder, k]
    sens_ref[...] = result


def local(mesh, now, before, courant, log, store, owner, cells, traces, weights):
    rows, ny, nz = courant.shape
    slabs, receivers = mesh.shape["slab"], mesh.shape["rcv"]
    xs = receivers // (ZHI * CORES)
    group = xs * CORES
    block = ny // group
    pairs = ZHI // CORES
    any_space = pl.BlockSpec(memory_space=pl.ANY)
    scalar = pl.BlockSpec(memory_space=pltpu.SMEM)
    dma = pltpu.SemaphoreType.DMA
    tall = ny + 2 * PAD
    return pl.pallas_call(
        functools.partial(kernel, (slabs, xs, ny, nz)),
        out_shape=(
            jax.ShapeDtypeStruct((rows, ny // receivers, nz), F32),
            jax.ShapeDtypeStruct(now.shape, F32),
        ),
        in_specs=[any_space] * 5 + [scalar] * 4,
        out_specs=(pl.BlockSpec(memory_space=pltpu.VMEM), any_space),
        scratch_shapes=[
            pltpu.VMEM((3, 3 * ROWS, tall, nz), F32),
            pltpu.VMEM((3 * ROWS, tall, nz), F32),
            pltpu.VMEM((3 * ROWS, ny, nz), F32),
            pltpu.VMEM((3, 3 * ROWS, ny, nz), F32),
            pltpu.VMEM((SNAPS, ROWS, ny, nz), F32),
            pltpu.VMEM((SNAPS, group - 1, ROWS, block, nz), F32),
            pltpu.VMEM((SNAPS, pairs, CORES, ROWS, 4, nz), F32),
            pltpu.VMEM((SNAPS, ZHI, ROWS, 4, nz), F32),
            pltpu.VMEM((group, ROWS, block, nz), F32),
            pltpu.VMEM((pairs, CORES, SNAPS, ROWS, 4, nz), F32),
            pltpu.VMEM((ZHI, SNAPS, ROWS, 4, nz), F32),
            dma((5,)),
            dma((3, 2)),
            dma((3, 2)),
            dma((SNAPS + 1, 2, CHUNKS)),
            dma((SNAPS + 1, 2, CHUNKS)),
            dma((SNAPS, group - 1)),
            dma((SNAPS, group - 1)),
            dma((SNAPS, pairs, CORES)),
            dma((SNAPS, ZHI)),
            dma((group - 1,)),
            dma((group - 1,)),
            dma((pairs, CORES)),
            dma((ZHI,)),
            dma((CHUNKS,)),
        ],
        compiler_params=pltpu.CompilerParams(
            collective_id=0, has_side_effects=True, vmem_limit_bytes=40 * 1024 * 1024
        ),
        name="adjoint",
    )(now, before, courant, log, store, owner, cells, traces, weights)


def solution(mesh):
    placed = (
        P("rcv", "slab", None, None),
        P("rcv", "slab", None, None),
        P("slab", None, None),
        P("slab", None, None),
        P("rcv", "slab", None, None),
        P(),
        P("rcv"),
        P("rcv", None),
        P("rcv"),
    )
    return jax.shard_map(
        functools.partial(local, mesh),
        mesh=mesh,
        in_specs=placed,
        out_specs=(P("slab", "rcv", None), P("rcv", "slab", None, None)),
        check_vma=False,
    )
```

```python
import functools

import jax
import jax.numpy as jnp
from jax import lax
from jax.experimental import pallas as pl
from jax.experimental.pallas import tpu as pltpu
from jax.sharding import PartitionSpec as P

MESH = pl.DeviceIdType.MESH
F32 = jnp.float32
SNAPS = 4
STEPS = 8
CORES = 2
ZHI = 4
ZLO = 4
ROWS = 4
CHUNKS = 8
PAD = 8
PARCELS = ((0, 4), (4, 7), (7, 8))
A, B, M = 0, 1, 2


def when(condition, action):
    pl.when(condition)(action)


def kernel(
    dims,
    now_ref,
    before_ref,
    courant_ref,
    log_ref,
    store_ref,
    owner_ref,
    cell_ref,
    trace_ref,
    weight_ref,
    sens_ref,
    after_ref,
    field,
    log_buf,
    courant,
    grad,
    weighted,
    group_in,
    snap_in,
    parcel_out,
    snap_tile,
    sum_tile,
    load_sem,
    model_send,
    model_recv,
    halo_send,
    halo_recv,
    group_send,
    group_recv,
    snap_send,
    snap_recv,
    parcel_send,
    parcel_recv,
    out_sem,
    relay,
):
    slabs, xs, ny, nz = dims
    group = xs * CORES
    block = ny // group
    pairs = ZHI // CORES
    chunk = ny // CHUNKS
    s = lax.axis_index("slab")
    r = lax.axis_index("rcv")
    core = lax.rem(r, CORES)
    zh = lax.rem(r // CORES, ZHI)
    xpos = r // (CORES * ZHI)
    member = xpos * CORES + core
    has_left, has_right = s > 0, s < slabs - 1

    def rcv_of(x, z, c):
        return (x * ZHI + z) * CORES + c

    def peer(d):
        other = lax.rem(member + d, group)
        return rcv_of(other // CORES, zh, lax.rem(other, CORES))

    barrier = pltpu.get_barrier_semaphore()

    def greet(slab, rcv):
        pl.semaphore_signal(barrier, 1, device_id=(slab, rcv), device_id_type=MESH)

    when(has_left, lambda: greet(s - 1, r))
    when(has_right, lambda: greet(s + 1, r))
    for d in range(1, group):
        greet(s, peer(d))
    half = zh // pairs

    columns = slabs // ZLO
    zline = zh * ZLO + s // columns
    length = ZHI * ZLO

    def along(d, c=core):
        z = lax.rem(zline + d + length, length)
        return lax.rem(z, ZLO) * columns + lax.rem(s, columns), rcv_of(xpos, z // ZLO, c)

    for d in (-1, 1):
        for c in range(CORES):
            greet(*along(d, c))

    def relay_signal(n):
        for d in (-(2**n), 2**n):
            pl.semaphore_signal(relay.at[n], 1, device_id=along(d), device_id_type=MESH)

    def relay_wait(n):
        pl.semaphore_wait(relay.at[n], 2)

    own = pl.ds(ROWS, ROWS)
    ycells = pl.ds(PAD, ny)
    loads = [
        pltpu.make_async_copy(log_ref, log_buf.at[own, ycells], load_sem.at[0]),
        pltpu.make_async_copy(courant_ref, courant.at[own], load_sem.at[1]),
        pltpu.make_async_copy(now_ref.at[0], field.at[A, own, ycells], load_sem.at[2]),
        pltpu.make_async_copy(before_ref.at[0], field.at[M, own, ycells], load_sem.at[3]),
        pltpu.make_async_copy(
            store_ref.at[0, :, pl.ds(pl.multiple_of(member * block, 8), block)],
            snap_in.at[group - 1],
            load_sem.at[4],
        ),
    ]
    for load in loads:
        load.start()

    zero_pad = jnp.zeros((3 * ROWS, PAD, nz), F32)
    for slot in (A, B, M):
        field[slot, :, 0:PAD, :] = zero_pad
        field[slot, :, PAD + ny : 2 * PAD + ny, :] = zero_pad
    log_buf[:, 0:PAD, :] = zero_pad
    log_buf[:, PAD + ny : 2 * PAD + ny, :] = zero_pad

    def clear(lo):
        def body(i, carry):
            rows = pl.ds(pl.multiple_of(i * 8, 8), 8)
            shifted = pl.ds(pl.multiple_of(i * 8 + PAD, 8), 8)
            zeros = jnp.zeros((8, nz), F32)
            for row in range(lo, lo + ROWS):
                for slot in (A, B, M):
                    field[slot, row, shifted, :] = zeros
                log_buf[row, shifted, :] = zeros
                courant[row, rows, :] = zeros
            return carry

        lax.fori_loop(0, ny // 8, body, 0)

    when(jnp.logical_not(has_left), lambda: clear(0))
    when(jnp.logical_not(has_right), lambda: clear(2 * ROWS))

    neighbours = has_left.astype(jnp.int32) + has_right.astype(jnp.int32)
    pl.semaphore_wait(barrier, neighbours + (group - 1) + 2 * CORES)

    def side_copy(side, src, dst, send, recv):
        return pltpu.make_async_remote_copy(
            src_ref=src,
            dst_ref=dst,
            send_sem=send,
            recv_sem=recv,
            device_id=(s + 1 if side == 0 else s - 1, r),
            device_id_type=MESH,
        )

    leaves = (has_right, has_left)
    comes = (has_left, has_right)

    def model_copy(which, side):
        near = (2, 0)[side]
        far = (0, 2)[side]
        land_near = (2, 8)[side]
        land_far = (0, 10)[side]
        part = pl.ds(pl.multiple_of(core * (ny // 2), 8), ny // 2)
        shifted = pl.ds(pl.multiple_of(core * (ny // 2) + PAD, 8), ny // 2)
        if which == 2:
            src, dst = courant_ref.at[near : near + 2, part], courant.at[land_near : land_near + 2, part]
        elif which == 1:
            src, dst = log_ref.at[far : far + 2, part], log_buf.at[land_far : land_far + 2, shifted]
        else:
            src, dst = log_ref.at[near : near + 2], log_buf.at[land_near : land_near + 2, ycells]
        return side_copy(side, src, dst, model_send.at[which, side], model_recv.at[which, side])

    def share_copy(which, side):
        part = pl.ds(pl.multiple_of(core * (ny // 2), 8), ny // 2)
        shifted = pl.ds(pl.multiple_of(core * (ny // 2) + PAD, 8), ny // 2)
        if which == 2:
            at = (2, 8)[side]
            block_ref = courant.at[at : at + 2, part]
        else:
            at = (0, 10)[side]
            block_ref = log_buf.at[at : at + 2, shifted]
        return pltpu.make_async_remote_copy(
            src_ref=block_ref,
            dst_ref=block_ref,
            send_sem=model_send.at[which + 2, side],
            recv_sem=model_recv.at[which + 2, side],
            device_id=(s, rcv_of(xpos, zh, 1 - core)),
            device_id_type=MESH,
        )

    def halo_copy(e, side, j, deep, slot, from_input=False):
        if deep == ROWS:
            at, to = 0, (0, 2 * ROWS)[side]
        else:
            at, to = (ROWS - deep, 0)[side], (ROWS - deep, 2 * ROWS)[side]
        here = pl.ds(pl.multiple_of(j * chunk, 8), chunk)
        there = pl.ds(pl.multiple_of(j * chunk + PAD, 8), chunk)
        if from_input:
            src = now_ref.at[0, at : at + deep, here]
        else:
            src = field.at[slot, ROWS + at : ROWS + at + deep, there]
        dst = field.at[slot, to : to + deep, there]
        return side_copy(side, src, dst, halo_send.at[e, side, j], halo_recv.at[e, side, j])

    def halo_start(e, j, deep, slot, from_input=False):
        for side in (0, 1):
            copy = halo_copy(e, side, j, deep, slot, from_input)
            when(leaves[side], copy.start)

    def halo_arrive(e, j, deep, slot):
        for side in (0, 1):
            copy = halo_copy(e, side, j, deep, slot)
            when(comes[side], copy.wait_recv)

    def halo_sent(e, deep, slot, from_input=False):
        def body(j, carry):
            for side in (0, 1):
                copy = halo_copy(e, side, j, deep, slot, from_input)
                when(leaves[side], copy.wait_send)
            return carry

        lax.fori_loop(0, CHUNKS, body, 0)

    for side in (0, 1):
        when(leaves[side], model_copy(0, side).start)
    for j in range(CHUNKS):
        halo_start(0, j, 2, A, True)
    relay_signal(0)

    def snap_copy(d):
        other = lax.rem(member + d, group)
        return pltpu.make_async_remote_copy(
            src_ref=store_ref.at[0, :, pl.ds(pl.multiple_of(other * block, 8), block)],
            dst_ref=snap_in.at[d - 1],
            send_sem=snap_send.at[d - 1],
            recv_sem=snap_recv.at[d - 1],
            device_id=(s, peer(d)),
            device_id_type=MESH,
        )

    for d in range(1, group):
        snap_copy(d).start()

    lane = lax.broadcasted_iota(jnp.int32, (8, nz), 1)
    ids = lax.broadcasted_iota(jnp.int32, (8, nz), 0) * nz + lane
    low1, low2 = lane >= 1, lane >= 2
    high1, high2 = lane < nz - 1, lane < nz - 2

    def z_shifts(u):
        zero = jnp.zeros_like(u)
        return (
            jnp.where(low2, pltpu.roll(u, 2, 1), zero),
            jnp.where(low1, pltpu.roll(u, 1, 1), zero),
            jnp.where(high1, pltpu.roll(u, nz - 1, 1), zero),
            jnp.where(high2, pltpu.roll(u, nz - 2, 1), zero),
        )

    twelfth = 1.0 / 12.0

    def slopes(rows):
        def body(i, carry):
            at = pl.ds(pl.multiple_of(i * 8, 8), 8)
            y0 = i * 8 + PAD
            mid = {}
            for row in rows:
                for k in (-2, -1, 0, 1, 2):
                    if row + k not in mid:
                        mid[row + k] = log_buf[row + k, pl.ds(pl.multiple_of(y0, 8), 8), :]
            results = []
            for row in rows:
                y = [log_buf[row, pl.ds(y0 + k, 8), :] for k in (-2, -1, 1, 2)]
                z = z_shifts(mid[row])
                x = [mid[row + k] for k in (-2, -1, 1, 2)]
                for axis, u in enumerate((x, y, z)):
                    slope = (8.0 * (u[2] - u[1]) - (u[3] - u[0])) * twelfth
                    results.append((axis, row, slope))
            scaled = [(row, courant[row, at, :] * twelfth) for row in rows]
            for axis, row, slope in results:
                grad[axis, row, at, :] = slope
            for row, value in scaled:
                courant[row, at, :] = value
            return carry

        lax.fori_loop(0, ny // 8, body, 0)

    cell = cell_ref[0]
    weight = weight_ref[0]

    def advance(dst, src, prev, rows, start, amplitude, snap=None, blocks=2):
        results = []
        for offset in range(blocks):
            i = start + offset
            at = pl.ds(pl.multiple_of(i * 8, 8), 8)
            y0 = i * 8 + PAD
            centre = pl.ds(pl.multiple_of(y0, 8), 8)
            mid = {row: field[src, row, centre, :] for row in range(rows[0] - 2, rows[-1] + 3)}
            for row in rows:
                u = mid[row]
                y = [field[src, row, pl.ds(y0 + k, 8), :] for k in (-2, -1, 1, 2)]
                z = z_shifts(u)
                x = [mid[row + k] for k in (-2, -1, 1, 2)]
                near = (x[1] + x[2]) + (y[1] + y[2]) + (z[1] + z[2])
                far = (x[0] + x[3]) + (y[0] + y[3]) + (z[0] + z[3])
                drift = [
                    grad[axis, row, at, :] * (8.0 * (v[2] - v[1]) - (v[3] - v[0]))
                    for axis, v in enumerate((x, y, z))
                ]
                change = (16.0 * near - far - 90.0 * u) + (drift[0] + drift[1] + drift[2])
                new = (2.0 * u - field[prev, row, centre, :]) + courant[row, at, :] * change
                base = ((s * ROWS + (row - ROWS)) * ny + i * 8) * nz
                new = new + jnp.where(ids == cell - base, amplitude, 0.0)
                results.append((row, at, centre, new))
        for row, at, centre, new in results:
            field[dst, row, centre, :] = new
            if snap is not None:
                weighted[snap, row - ROWS, at, :] = weight * new

    own_rows = range(ROWS, 2 * ROWS)
    wide_rows = range(ROWS - 2, 2 * ROWS + 2)
    per = chunk // 16

    def group_copy(k, other):
        d = lax.rem(other - member + group, group)
        return d, pltpu.make_async_remote_copy(
            src_ref=weighted.at[k, :, pl.ds(pl.multiple_of(other * block, 8), block)],
            dst_ref=group_in.at[k, jnp.maximum(d - 1, 0)],
            send_sem=group_send.at[k, jnp.maximum(d - 1, 0)],
            recv_sem=group_recv.at[k, jnp.maximum(d - 1, 0)],
            device_id=(s, rcv_of(other // CORES, zh, lax.rem(other, CORES))),
            device_id_type=MESH,
        )

    def group_start(k, j):
        for other in range(group // CHUNKS):
            d, copy = group_copy(k, j * (group // CHUNKS) + other)
            when(d > 0, copy.start)

    def group_wait(k, arrival):
        for d in range(1, group):
            copy = group_copy(k, lax.rem(member + d, group))[1]
            if arrival:
                copy.wait_recv()
            else:
                copy.wait_send()

    pieces = [(i, c, (2 * i + c) * 4) for i in range(pairs) for c in range(CORES)]

    def landing(part, z):
        lo, hi = PARCELS[part]
        return snap_tile.at[z] if part == 0 else sum_tile.at[z, lo - SNAPS : hi - SNAPS]

    def parcel_copy(part, i, c):
        lo, hi = PARCELS[part]
        z = core * pairs + i
        return (z == zh) & (c == core), pltpu.make_async_remote_copy(
            src_ref=parcel_out.at[i, c, lo:hi],
            dst_ref=landing(part, zh),
            send_sem=parcel_send.at[part, i, c],
            recv_sem=parcel_recv.at[part, zh],
            device_id=(s, rcv_of(xpos, z, c)),
            device_id_type=MESH,
        )

    def parcel_start(part):
        lo, hi = PARCELS[part]
        for i, c, at in pieces:
            to_self, copy = parcel_copy(part, i, c)
            when(jnp.logical_not(to_self), copy.start)

            @pl.when(to_self)
            def _():
                for n in range(lo, hi):
                    landing(part, zh)[n - lo] = parcel_out[i, c, n]

    def parcel_sent(part):
        for i, c, at in pieces:
            to_self, copy = parcel_copy(part, i, c)
            when(jnp.logical_not(to_self), copy.wait_send)

    def parcel_arrive(part):
        for z in range(ZHI):
            copy = pltpu.make_async_remote_copy(
                src_ref=landing(part, z),
                dst_ref=landing(part, z),
                send_sem=parcel_recv.at[part, z],
                recv_sem=parcel_recv.at[part, z],
                device_id=(s, rcv_of(xpos, z, half)),
                device_id_type=MESH,
            )
            when((z != zh) | (half != core), copy.wait_recv)

    def sum_tiles(k):
        group_wait(k, True)
        results = []
        for i, c, at in pieces:
            for row in range(ROWS):
                terms = [weighted[k, row, pl.ds(member * block + at, 4), :]]
                terms += [group_in[k, d, row, at : at + 4, :] for d in range(group - 1)]
                while len(terms) > 1:
                    terms = [a + b for a, b in zip(terms[::2], terms[1::2])]
                results.append((i, c, row, terms[0]))
        for i, c, row, total in results:
            parcel_out[i, c, SNAPS + k, row] = total

    def snap_tiles():
        loads[4].wait()
        for d in range(1, group):
            snap_copy(d).wait_recv()
        for k in range(SNAPS):
            slot = owner_ref[k]
            holder = (slot // (CORES * ZHI)) * CORES + lax.rem(slot, CORES)
            place = lax.rem(member - holder + 2 * group - 1, group)
            results = [
                (i, c, row, snap_in[place, row, at : at + 4, :])
                for i, c, at in pieces
                for row in range(ROWS)
            ]
            for i, c, row, value in results:
                parcel_out[i, c, k, row] = value

    loads[0].wait()
    loads[1].wait()
    for side in (0, 1):
        when(comes[side], model_copy(0, side).wait_recv)
    slopes(own_rows)
    loads[2].wait()
    loads[3].wait()
    relay_wait(0)
    relay_signal(1)

    def first(j, carry):
        halo_arrive(0, j, 2, A)

        def body(i, inner):
            advance(M, A, M, own_rows, 2 * i, trace_ref[0, 0])
            return inner

        lax.fori_loop(j * per, (j + 1) * per, body, 0)
        halo_start(1, j, 2, M)
        return carry

    lax.fori_loop(0, CHUNKS, first, 0)
    for which in (1, 2):
        for side in (0, 1):
            when(leaves[side], model_copy(which, side).start)
    relay_wait(1)
    relay_signal(2)

    def second(j, carry):
        halo_arrive(1, j, 2, M)

        def body(i, inner):
            advance(B, M, A, own_rows, 2 * i, trace_ref[0, 1], 0)
            return inner

        lax.fori_loop(j * per, (j + 1) * per, body, 0)
        halo_start(2, j, ROWS, B)
        group_start(0, j)
        return carry

    lax.fori_loop(0, CHUNKS, second, 0)
    for which in (1, 2):
        for side in (0, 1):
            when(comes[side], model_copy(which, side).wait_recv)
            when(comes[side], share_copy(which, side).start)
    snap_tiles()
    relay_wait(2)
    parcel_start(0)
    for which in (1, 2):
        for side in (0, 1):
            when(comes[side], share_copy(which, side).wait)
    slopes((2, 3, 8, 9))
    halo_sent(0, 2, A, True)
    halo_sent(1, 2, M)

    def pair(p, carry):
        src = lax.rem(p, 2)
        dst = 1 - src

        @pl.when(p > 1)
        def _():
            halo_sent(p, ROWS, dst)

        def part(j, inner):
            @pl.when(j == 0)
            def _():
                halo_arrive(p + 1, 0, ROWS, src)

            @pl.when(j < CHUNKS - 1)
            def _():
                halo_arrive(p + 1, j + 1, ROWS, src)

            def middle(start, blocks):
                advance(M, src, M, wide_rows, start, trace_ref[0, 2 * p], None, blocks)

            when(j == 0, lambda: middle(0, 1))

            def ahead(i, deep):
                when(i < ny // 16 - 1, lambda: middle(2 * i + 1, 2))
                when(i == ny // 16 - 1, lambda: middle(2 * i + 1, 1))
                return deep

            lax.fori_loop(j * per, (j + 1) * per, ahead, 0)

            def final(i, deep):
                advance(dst, M, src, own_rows, 2 * i, trace_ref[0, 2 * p + 1], p)
                return deep

            lax.fori_loop(j * per, (j + 1) * per, final, 0)
            when(p < SNAPS - 1, lambda: halo_start(p + 2, j, ROWS, dst))
            group_start(p, j)

            @pl.when((p == SNAPS - 1) & (j == CHUNKS - 2))
            def _():
                for k in range(SNAPS - 1):
                    sum_tiles(k)
                parcel_start(1)

            @pl.when(p == SNAPS - 1)
            def _():
                at = pl.ds(pl.multiple_of(j * chunk, 8), chunk)
                there = pl.ds(pl.multiple_of(j * chunk + PAD, 8), chunk)
                pltpu.make_async_copy(
                    field.at[dst, own, there], after_ref.at[0, :, at], out_sem.at[j]
                ).start()

            return inner

        lax.fori_loop(0, CHUNKS, part, 0)
        return carry

    lax.fori_loop(1, SNAPS, pair, 0)
    sum_tiles(SNAPS - 1)
    parcel_start(2)

    halo_sent(SNAPS, ROWS, B)
    for which in range(3):
        for side in (0, 1):
            when(leaves[side], model_copy(which, side).wait_send)
    for d in range(1, group):
        snap_copy(d).wait_send()
    for k in range(SNAPS):
        group_wait(k, False)
    for j in range(CHUNKS):
        at = pl.ds(j * chunk, chunk)
        there = pl.ds(j * chunk + PAD, chunk)
        pltpu.make_async_copy(field.at[A, own, there], after_ref.at[0, :, at], out_sem.at[j]).wait()

    def kernel_term(k):
        total = (sum_tile[0, k] + sum_tile[1, k]) + (sum_tile[2, k] + sum_tile[3, k])
        holder = lax.rem(owner_ref[k] // CORES, ZHI)
        return total * snap_tile[holder, k]

    parcel_sent(0)
    parcel_sent(1)
    parcel_arrive(0)
    parcel_arrive(1)
    early = (kernel_term(0) + kernel_term(1)) + kernel_term(2)
    parcel_arrive(2)
    sens_ref[...] = early + kernel_term(SNAPS - 1)
    parcel_sent(2)


def local(mesh, now, before, courant, log, store, owner, cells, traces, weights):
    rows, ny, nz = courant.shape
    slabs, receivers = mesh.shape["slab"], mesh.shape["rcv"]
    xs = receivers // (ZHI * CORES)
    group = xs * CORES
    block = ny // group
    pairs = ZHI // CORES
    any_space = pl.BlockSpec(memory_space=pltpu.HBM)
    scalar = pl.BlockSpec(memory_space=pltpu.SMEM)
    dma = pltpu.SemaphoreType.DMA
    tall = ny + 2 * PAD
    return pl.pallas_call(
        functools.partial(kernel, (slabs, xs, ny, nz)),
        out_shape=(
            jax.ShapeDtypeStruct((rows, ny // receivers, nz), F32),
            jax.ShapeDtypeStruct(now.shape, F32),
        ),
        in_specs=[any_space] * 5 + [scalar] * 4,
        out_specs=(pl.BlockSpec(memory_space=pltpu.VMEM), any_space),
        scratch_shapes=[
            pltpu.VMEM((3, 3 * ROWS, tall, nz), F32),
            pltpu.VMEM((3 * ROWS, tall, nz), F32),
            pltpu.VMEM((3 * ROWS, ny, nz), F32),
            pltpu.VMEM((3, 3 * ROWS, ny, nz), F32),
            pltpu.VMEM((SNAPS, ROWS, ny, nz), F32),
            pltpu.VMEM((SNAPS, group - 1, ROWS, block, nz), F32),
            pltpu.VMEM((group, ROWS, block, nz), F32),
            pltpu.VMEM((pairs, CORES, 2 * SNAPS, ROWS, 4, nz), F32),
            pltpu.VMEM((ZHI, SNAPS, ROWS, 4, nz), F32),
            pltpu.VMEM((ZHI, SNAPS, ROWS, 4, nz), F32),
            dma((5,)),
            dma((5, 2)),
            dma((5, 2)),
            dma((SNAPS + 1, 2, CHUNKS)),
            dma((SNAPS + 1, 2, CHUNKS)),
            dma((SNAPS, group - 1)),
            dma((SNAPS, group - 1)),
            dma((group - 1,)),
            dma((group - 1,)),
            dma((len(PARCELS), pairs, CORES)),
            dma((len(PARCELS), ZHI)),
            dma((CHUNKS,)),
            pltpu.SemaphoreType.REGULAR((3,)),
        ],
        compiler_params=pltpu.CompilerParams(
            collective_id=0, has_side_effects=True, vmem_limit_bytes=60 * 1024 * 1024
        ),
        name="adjoint",
    )(now, before, courant, log, store, owner, cells, traces, weights)


def solution(mesh):
    placed = (
        P("rcv", "slab", None, None),
        P("rcv", "slab", None, None),
        P("slab", None, None),
        P("slab", None, None),
        P("rcv", "slab", None, None),
        P(),
        P("rcv"),
        P("rcv", None),
        P("rcv"),
    )
    return jax.shard_map(
        functools.partial(local, mesh),
        mesh=mesh,
        in_specs=placed,
        out_specs=(P("slab", "rcv", None), P("rcv", "slab", None, None)),
        check_vma=False,
    )
```

```python
import functools

import jax
import jax.numpy as jnp
from jax import lax
from jax.experimental import pallas as pl
from jax.experimental.pallas import tpu as pltpu
from jax.sharding import PartitionSpec as P

MESH = pl.DeviceIdType.MESH
F32 = jnp.float32
SNAPS = 4
STEPS = 8
CORES = 2
ZHI = 4
ZLO = 4
ROWS = 4
CHUNKS = 8
PAD = 8
PARCELS = ((0, 4), (4, 7), (7, 8))
A, B, M = 0, 1, 2


def when(condition, action):
    pl.when(condition)(action)


def kernel(
    dims,
    now_ref,
    before_ref,
    courant_ref,
    log_ref,
    store_ref,
    owner_ref,
    cell_ref,
    trace_ref,
    weight_ref,
    sens_ref,
    after_ref,
    field,
    log_buf,
    courant,
    grad,
    weighted,
    group_in,
    snap_in,
    parcel_out,
    snap_tile,
    sum_tile,
    load_sem,
    model_send,
    model_recv,
    halo_send,
    halo_recv,
    group_send,
    group_recv,
    snap_send,
    snap_recv,
    parcel_send,
    parcel_recv,
    out_sem,
    relay,
):
    slabs, xs, ny, nz = dims
    group = xs * CORES
    block = ny // group
    pairs = ZHI // CORES
    chunk = ny // CHUNKS
    s = lax.axis_index("slab")
    r = lax.axis_index("rcv")
    core = lax.rem(r, CORES)
    zh = lax.rem(r // CORES, ZHI)
    xpos = r // (CORES * ZHI)
    member = xpos * CORES + core
    has_left, has_right = s > 0, s < slabs - 1

    def rcv_of(x, z, c):
        return (x * ZHI + z) * CORES + c

    def peer(d):
        other = lax.rem(member + d, group)
        return rcv_of(other // CORES, zh, lax.rem(other, CORES))

    barrier = pltpu.get_barrier_semaphore()

    def greet(slab, rcv):
        pl.semaphore_signal(barrier, 1, device_id=(slab, rcv), device_id_type=MESH)

    when(has_left, lambda: greet(s - 1, r))
    when(has_right, lambda: greet(s + 1, r))
    for d in range(1, group):
        greet(s, peer(d))
    half = zh // pairs

    columns = slabs // ZLO
    zline = zh * ZLO + s // columns
    length = ZHI * ZLO

    def along(d, c=core):
        z = lax.rem(zline + d + length, length)
        return lax.rem(z, ZLO) * columns + lax.rem(s, columns), rcv_of(xpos, z // ZLO, c)

    for d in (-1, 1):
        for c in range(CORES):
            greet(*along(d, c))

    def relay_signal(n):
        for d in (-(2**n), 2**n):
            pl.semaphore_signal(relay.at[n], 1, device_id=along(d), device_id_type=MESH)

    def relay_wait(n):
        pl.semaphore_wait(relay.at[n], 2)

    own = pl.ds(ROWS, ROWS)
    ycells = pl.ds(PAD, ny)
    loads = [
        pltpu.make_async_copy(log_ref, log_buf.at[own, ycells], load_sem.at[0]),
        pltpu.make_async_copy(courant_ref, courant.at[own], load_sem.at[1]),
        pltpu.make_async_copy(now_ref.at[0], field.at[A, own, ycells], load_sem.at[2]),
        pltpu.make_async_copy(before_ref.at[0], field.at[M, own, ycells], load_sem.at[3]),
        pltpu.make_async_copy(
            store_ref.at[0, :, pl.ds(pl.multiple_of(member * block, 8), block)],
            snap_in.at[group - 1],
            load_sem.at[4],
        ),
    ]
    for load in loads:
        load.start()

    zero_pad = jnp.zeros((3 * ROWS, PAD, nz), F32)
    for slot in (A, B, M):
        field[slot, :, 0:PAD, :] = zero_pad
        field[slot, :, PAD + ny : 2 * PAD + ny, :] = zero_pad
    log_buf[:, 0:PAD, :] = zero_pad
    log_buf[:, PAD + ny : 2 * PAD + ny, :] = zero_pad

    def clear(lo):
        def body(i, carry):
            rows = pl.ds(pl.multiple_of(i * 8, 8), 8)
            shifted = pl.ds(pl.multiple_of(i * 8 + PAD, 8), 8)
            zeros = jnp.zeros((8, nz), F32)
            for row in range(lo, lo + ROWS):
                for slot in (A, B, M):
                    field[slot, row, shifted, :] = zeros
                log_buf[row, shifted, :] = zeros
                courant[row, rows, :] = zeros
            return carry

        lax.fori_loop(0, ny // 8, body, 0)

    when(jnp.logical_not(has_left), lambda: clear(0))
    when(jnp.logical_not(has_right), lambda: clear(2 * ROWS))

    neighbours = has_left.astype(jnp.int32) + has_right.astype(jnp.int32)
    pl.semaphore_wait(barrier, neighbours + (group - 1) + 2 * CORES)

    def side_copy(side, src, dst, send, recv):
        return pltpu.make_async_remote_copy(
            src_ref=src,
            dst_ref=dst,
            send_sem=send,
            recv_sem=recv,
            device_id=(s + 1 if side == 0 else s - 1, r),
            device_id_type=MESH,
        )

    leaves = (has_right, has_left)
    comes = (has_left, has_right)

    def model_copy(which, side):
        near = (2, 0)[side]
        far = (0, 2)[side]
        land_near = (2, 8)[side]
        land_far = (0, 10)[side]
        part = pl.ds(pl.multiple_of(core * (ny // 2), 8), ny // 2)
        shifted = pl.ds(pl.multiple_of(core * (ny // 2) + PAD, 8), ny // 2)
        if which == 2:
            src, dst = courant_ref.at[near : near + 2, part], courant.at[land_near : land_near + 2, part]
        else:
            at, to = ((near, land_near), (far, land_far))[which]
            src, dst = log_ref.at[at : at + 2, part], log_buf.at[to : to + 2, shifted]
        return side_copy(side, src, dst, model_send.at[which, side], model_recv.at[which, side])

    def share_copy(which, side):
        part = pl.ds(pl.multiple_of(core * (ny // 2), 8), ny // 2)
        shifted = pl.ds(pl.multiple_of(core * (ny // 2) + PAD, 8), ny // 2)
        if which == 2:
            at = (2, 8)[side]
            block_ref = courant.at[at : at + 2, part]
        else:
            at = ((2, 8), (0, 10))[which][side]
            block_ref = log_buf.at[at : at + 2, shifted]
        return pltpu.make_async_remote_copy(
            src_ref=block_ref,
            dst_ref=block_ref,
            send_sem=model_send.at[which + 3, side],
            recv_sem=model_recv.at[which + 3, side],
            device_id=(s, rcv_of(xpos, zh, 1 - core)),
            device_id_type=MESH,
        )

    def share_start(which):
        for side in (0, 1):
            when(comes[side], model_copy(which, side).wait_recv)
            when(comes[side], share_copy(which, side).start)

    def share_wait(which):
        for side in (0, 1):
            when(comes[side], share_copy(which, side).wait)

    def halo_copy(e, side, j, deep, slot, from_input=False):
        if deep == ROWS:
            at, to = 0, (0, 2 * ROWS)[side]
        else:
            at, to = (ROWS - deep, 0)[side], (ROWS - deep, 2 * ROWS)[side]
        here = pl.ds(pl.multiple_of(j * chunk, 8), chunk)
        there = pl.ds(pl.multiple_of(j * chunk + PAD, 8), chunk)
        if from_input:
            src = now_ref.at[0, at : at + deep, here]
        else:
            src = field.at[slot, ROWS + at : ROWS + at + deep, there]
        dst = field.at[slot, to : to + deep, there]
        return side_copy(side, src, dst, halo_send.at[e, side, j], halo_recv.at[e, side, j])

    def halo_start(e, j, deep, slot, from_input=False):
        for side in (0, 1):
            copy = halo_copy(e, side, j, deep, slot, from_input)
            when(leaves[side], copy.start)

    def halo_arrive(e, j, deep, slot):
        for side in (0, 1):
            copy = halo_copy(e, side, j, deep, slot)
            when(comes[side], copy.wait_recv)

    def halo_sent(e, deep, slot, from_input=False):
        def body(j, carry):
            for side in (0, 1):
                copy = halo_copy(e, side, j, deep, slot, from_input)
                when(leaves[side], copy.wait_send)
            return carry

        lax.fori_loop(0, CHUNKS, body, 0)

    for side in (0, 1):
        when(leaves[side], model_copy(0, side).start)
    for j in range(CHUNKS):
        halo_start(0, j, 2, A, True)
    for which in (1, 2):
        for side in (0, 1):
            when(leaves[side], model_copy(which, side).start)
    relay_signal(0)

    def snap_copy(d):
        other = lax.rem(member + d, group)
        return pltpu.make_async_remote_copy(
            src_ref=store_ref.at[0, :, pl.ds(pl.multiple_of(other * block, 8), block)],
            dst_ref=snap_in.at[d - 1],
            send_sem=snap_send.at[d - 1],
            recv_sem=snap_recv.at[d - 1],
            device_id=(s, peer(d)),
            device_id_type=MESH,
        )

    lane = lax.broadcasted_iota(jnp.int32, (8, nz), 1)
    ids = lax.broadcasted_iota(jnp.int32, (8, nz), 0) * nz + lane
    low1, low2 = lane >= 1, lane >= 2
    high1, high2 = lane < nz - 1, lane < nz - 2

    def z_shifts(u):
        zero = jnp.zeros_like(u)
        return (
            jnp.where(low2, pltpu.roll(u, 2, 1), zero),
            jnp.where(low1, pltpu.roll(u, 1, 1), zero),
            jnp.where(high1, pltpu.roll(u, nz - 1, 1), zero),
            jnp.where(high2, pltpu.roll(u, nz - 2, 1), zero),
        )

    twelfth = 1.0 / 12.0

    def slopes(rows):
        def body(i, carry):
            at = pl.ds(pl.multiple_of(i * 8, 8), 8)
            y0 = i * 8 + PAD
            mid = {}
            for row in rows:
                for k in (-2, -1, 0, 1, 2):
                    if row + k not in mid:
                        mid[row + k] = log_buf[row + k, pl.ds(pl.multiple_of(y0, 8), 8), :]
            results = []
            for row in rows:
                y = [log_buf[row, pl.ds(y0 + k, 8), :] for k in (-2, -1, 1, 2)]
                z = z_shifts(mid[row])
                x = [mid[row + k] for k in (-2, -1, 1, 2)]
                for axis, u in enumerate((x, y, z)):
                    slope = (8.0 * (u[2] - u[1]) - (u[3] - u[0])) * twelfth
                    results.append((axis, row, slope))
            scaled = [(row, courant[row, at, :] * twelfth) for row in rows]
            for axis, row, slope in results:
                grad[axis, row, at, :] = slope
            for row, value in scaled:
                courant[row, at, :] = value
            return carry

        lax.fori_loop(0, ny // 8, body, 0)

    cell = cell_ref[0]
    weight = weight_ref[0]

    def advance(dst, src, prev, rows, start, amplitude, snap=None, blocks=2):
        results = []
        for offset in range(blocks):
            i = start + offset
            at = pl.ds(pl.multiple_of(i * 8, 8), 8)
            y0 = i * 8 + PAD
            centre = pl.ds(pl.multiple_of(y0, 8), 8)
            mid = {row: field[src, row, centre, :] for row in range(rows[0] - 2, rows[-1] + 3)}
            for row in rows:
                u = mid[row]
                y = [field[src, row, pl.ds(y0 + k, 8), :] for k in (-2, -1, 1, 2)]
                z = z_shifts(u)
                x = [mid[row + k] for k in (-2, -1, 1, 2)]
                near = (x[1] + x[2]) + (y[1] + y[2]) + (z[1] + z[2])
                far = (x[0] + x[3]) + (y[0] + y[3]) + (z[0] + z[3])
                drift = [
                    grad[axis, row, at, :] * (8.0 * (v[2] - v[1]) - (v[3] - v[0]))
                    for axis, v in enumerate((x, y, z))
                ]
                change = (16.0 * near - far - 90.0 * u) + (drift[0] + drift[1] + drift[2])
                new = (2.0 * u - field[prev, row, centre, :]) + courant[row, at, :] * change
                base = ((s * ROWS + (row - ROWS)) * ny + i * 8) * nz
                new = new + jnp.where(ids == cell - base, amplitude, 0.0)
                results.append((row, at, centre, new))
        for row, at, centre, new in results:
            field[dst, row, centre, :] = new
            if snap is not None:
                weighted[snap, row - ROWS, at, :] = weight * new

    own_rows = range(ROWS, 2 * ROWS)
    wide_rows = range(ROWS - 2, 2 * ROWS + 2)
    per = chunk // 16

    def group_copy(k, other):
        d = lax.rem(other - member + group, group)
        return d, pltpu.make_async_remote_copy(
            src_ref=weighted.at[k, :, pl.ds(pl.multiple_of(other * block, 8), block)],
            dst_ref=group_in.at[k, jnp.maximum(d - 1, 0)],
            send_sem=group_send.at[k, jnp.maximum(d - 1, 0)],
            recv_sem=group_recv.at[k, jnp.maximum(d - 1, 0)],
            device_id=(s, rcv_of(other // CORES, zh, lax.rem(other, CORES))),
            device_id_type=MESH,
        )

    def group_start(k, j):
        for other in range(group // CHUNKS):
            d, copy = group_copy(k, j * (group // CHUNKS) + other)
            when(d > 0, copy.start)

    def group_wait(k, arrival):
        for d in range(1, group):
            copy = group_copy(k, lax.rem(member + d, group))[1]
            if arrival:
                copy.wait_recv()
            else:
                copy.wait_send()

    pieces = [(i, c, (2 * i + c) * 4) for i in range(pairs) for c in range(CORES)]

    def landing(part, z):
        lo, hi = PARCELS[part]
        return snap_tile.at[z] if part == 0 else sum_tile.at[z, lo - SNAPS : hi - SNAPS]

    def parcel_copy(part, i, c):
        lo, hi = PARCELS[part]
        z = core * pairs + i
        return (z == zh) & (c == core), pltpu.make_async_remote_copy(
            src_ref=parcel_out.at[i, c, lo:hi],
            dst_ref=landing(part, zh),
            send_sem=parcel_send.at[part, i, c],
            recv_sem=parcel_recv.at[part, zh],
            device_id=(s, rcv_of(xpos, z, c)),
            device_id_type=MESH,
        )

    def parcel_start(part):
        lo, hi = PARCELS[part]
        for i, c, at in pieces:
            to_self, copy = parcel_copy(part, i, c)
            when(jnp.logical_not(to_self), copy.start)

            @pl.when(to_self)
            def _():
                for n in range(lo, hi):
                    landing(part, zh)[n - lo] = parcel_out[i, c, n]

    def parcel_sent(part):
        for i, c, at in pieces:
            to_self, copy = parcel_copy(part, i, c)
            when(jnp.logical_not(to_self), copy.wait_send)

    def parcel_arrive(part):
        for z in range(ZHI):
            copy = pltpu.make_async_remote_copy(
                src_ref=landing(part, z),
                dst_ref=landing(part, z),
                send_sem=parcel_recv.at[part, z],
                recv_sem=parcel_recv.at[part, z],
                device_id=(s, rcv_of(xpos, z, half)),
                device_id_type=MESH,
            )
            when((z != zh) | (half != core), copy.wait_recv)

    def sum_tiles(k):
        group_wait(k, True)
        results = []
        for i, c, at in pieces:
            for row in range(ROWS):
                terms = [weighted[k, row, pl.ds(member * block + at, 4), :]]
                terms += [group_in[k, d, row, at : at + 4, :] for d in range(group - 1)]
                while len(terms) > 1:
                    terms = [a + b for a, b in zip(terms[::2], terms[1::2])]
                results.append((i, c, row, terms[0]))
        for i, c, row, total in results:
            parcel_out[i, c, SNAPS + k, row] = total

    def snap_tiles():
        loads[4].wait()
        for d in range(1, group):
            snap_copy(d).wait_recv()
        for k in range(SNAPS):
            slot = owner_ref[k]
            holder = (slot // (CORES * ZHI)) * CORES + lax.rem(slot, CORES)
            place = lax.rem(member - holder + 2 * group - 1, group)
            results = [
                (i, c, row, snap_in[place, row, at : at + 4, :])
                for i, c, at in pieces
                for row in range(ROWS)
            ]
            for i, c, row, value in results:
                parcel_out[i, c, k, row] = value

    loads[0].wait()
    loads[1].wait()
    share_start(0)
    share_wait(0)
    slopes(own_rows)
    for d in range(1, group):
        snap_copy(d).start()
    loads[2].wait()
    loads[3].wait()
    relay_wait(0)
    relay_signal(1)

    def first(j, carry):
        halo_arrive(0, j, 2, A)

        def body(i, inner):
            advance(M, A, M, own_rows, 2 * i, trace_ref[0, 0])
            return inner

        lax.fori_loop(j * per, (j + 1) * per, body, 0)
        halo_start(1, j, 2, M)
        return carry

    lax.fori_loop(0, CHUNKS, first, 0)
    for which in (1, 2):
        share_start(which)
    relay_wait(1)
    relay_signal(2)

    def second(j, carry):
        halo_arrive(1, j, 2, M)

        def body(i, inner):
            advance(B, M, A, own_rows, 2 * i, trace_ref[0, 1], 0)
            return inner

        lax.fori_loop(j * per, (j + 1) * per, body, 0)
        halo_start(2, j, ROWS, B)
        group_start(0, j)
        return carry

    lax.fori_loop(0, CHUNKS, second, 0)
    for which in (1, 2):
        share_wait(which)
    slopes((2, 3, 8, 9))
    snap_tiles()
    relay_wait(2)
    parcel_start(0)
    halo_sent(0, 2, A, True)
    halo_sent(1, 2, M)

    def pair(p, carry):
        src = lax.rem(p, 2)
        dst = 1 - src

        @pl.when(p > 1)
        def _():
            halo_sent(p, ROWS, dst)

        def part(j, inner):
            @pl.when((p == SNAPS - 1) & (j == 0))
            def _():
                for k in range(SNAPS - 2):
                    sum_tiles(k)

            @pl.when(j == 0)
            def _():
                halo_arrive(p + 1, 0, ROWS, src)

            @pl.when(j < CHUNKS - 1)
            def _():
                halo_arrive(p + 1, j + 1, ROWS, src)

            def middle(start, blocks):
                advance(M, src, M, wide_rows, start, trace_ref[0, 2 * p], None, blocks)

            when(j == 0, lambda: middle(0, 1))

            def ahead(i, deep):
                when(i < ny // 16 - 1, lambda: middle(2 * i + 1, 2))
                when(i == ny // 16 - 1, lambda: middle(2 * i + 1, 1))
                return deep

            lax.fori_loop(j * per, (j + 1) * per, ahead, 0)

            def final(i, deep):
                advance(dst, M, src, own_rows, 2 * i, trace_ref[0, 2 * p + 1], p)
                return deep

            lax.fori_loop(j * per, (j + 1) * per, final, 0)
            when(p < SNAPS - 1, lambda: halo_start(p + 2, j, ROWS, dst))
            group_start(p, j)

            @pl.when((p == SNAPS - 1) & (j == CHUNKS - 2))
            def _():
                sum_tiles(SNAPS - 2)
                parcel_start(1)

            @pl.when(p == SNAPS - 1)
            def _():
                at = pl.ds(pl.multiple_of(j * chunk, 8), chunk)
                there = pl.ds(pl.multiple_of(j * chunk + PAD, 8), chunk)
                pltpu.make_async_copy(
                    field.at[dst, own, there], after_ref.at[0, :, at], out_sem.at[j]
                ).start()

            return inner

        lax.fori_loop(0, CHUNKS, part, 0)
        return carry

    lax.fori_loop(1, SNAPS, pair, 0)
    sum_tiles(SNAPS - 1)
    parcel_start(2)

    halo_sent(SNAPS, ROWS, B)
    for which in range(3):
        for side in (0, 1):
            when(leaves[side], model_copy(which, side).wait_send)
    for d in range(1, group):
        snap_copy(d).wait_send()
    for k in range(SNAPS):
        group_wait(k, False)
    for j in range(CHUNKS):
        at = pl.ds(j * chunk, chunk)
        there = pl.ds(j * chunk + PAD, chunk)
        pltpu.make_async_copy(field.at[A, own, there], after_ref.at[0, :, at], out_sem.at[j]).wait()

    def kernel_term(k):
        total = (sum_tile[0, k] + sum_tile[1, k]) + (sum_tile[2, k] + sum_tile[3, k])
        holder = lax.rem(owner_ref[k] // CORES, ZHI)
        return total * snap_tile[holder, k]

    parcel_sent(0)
    parcel_sent(1)
    parcel_arrive(0)
    parcel_arrive(1)
    early = (kernel_term(0) + kernel_term(1)) + kernel_term(2)
    parcel_arrive(2)
    sens_ref[...] = early + kernel_term(SNAPS - 1)
    parcel_sent(2)


def local(mesh, now, before, courant, log, store, owner, cells, traces, weights):
    rows, ny, nz = courant.shape
    slabs, receivers = mesh.shape["slab"], mesh.shape["rcv"]
    xs = receivers // (ZHI * CORES)
    group = xs * CORES
    block = ny // group
    pairs = ZHI // CORES
    any_space = pl.BlockSpec(memory_space=pltpu.HBM)
    scalar = pl.BlockSpec(memory_space=pltpu.SMEM)
    dma = pltpu.SemaphoreType.DMA
    tall = ny + 2 * PAD
    return pl.pallas_call(
        functools.partial(kernel, (slabs, xs, ny, nz)),
        out_shape=(
            jax.ShapeDtypeStruct((rows, ny // receivers, nz), F32),
            jax.ShapeDtypeStruct(now.shape, F32),
        ),
        in_specs=[any_space] * 5 + [scalar] * 4,
        out_specs=(pl.BlockSpec(memory_space=pltpu.VMEM), any_space),
        scratch_shapes=[
            pltpu.VMEM((3, 3 * ROWS, tall, nz), F32),
            pltpu.VMEM((3 * ROWS, tall, nz), F32),
            pltpu.VMEM((3 * ROWS, ny, nz), F32),
            pltpu.VMEM((3, 3 * ROWS, ny, nz), F32),
            pltpu.VMEM((SNAPS, ROWS, ny, nz), F32),
            pltpu.VMEM((SNAPS, group - 1, ROWS, block, nz), F32),
            pltpu.VMEM((group, ROWS, block, nz), F32),
            pltpu.VMEM((pairs, CORES, 2 * SNAPS, ROWS, 4, nz), F32),
            pltpu.VMEM((ZHI, SNAPS, ROWS, 4, nz), F32),
            pltpu.VMEM((ZHI, SNAPS, ROWS, 4, nz), F32),
            dma((5,)),
            dma((6, 2)),
            dma((6, 2)),
            dma((SNAPS + 1, 2, CHUNKS)),
            dma((SNAPS + 1, 2, CHUNKS)),
            dma((SNAPS, group - 1)),
            dma((SNAPS, group - 1)),
            dma((group - 1,)),
            dma((group - 1,)),
            dma((len(PARCELS), pairs, CORES)),
            dma((len(PARCELS), ZHI)),
            dma((CHUNKS,)),
            pltpu.SemaphoreType.REGULAR((3,)),
        ],
        compiler_params=pltpu.CompilerParams(
            collective_id=0, has_side_effects=True, vmem_limit_bytes=60 * 1024 * 1024
        ),
        name="adjoint",
    )(now, before, courant, log, store, owner, cells, traces, weights)


def solution(mesh):
    placed = (
        P("rcv", "slab", None, None),
        P("rcv", "slab", None, None),
        P("slab", None, None),
        P("slab", None, None),
        P("rcv", "slab", None, None),
        P(),
        P("rcv"),
        P("rcv", None),
        P("rcv"),
    )
    return jax.shard_map(
        functools.partial(local, mesh),
        mesh=mesh,
        in_specs=placed,
        out_specs=(P("slab", "rcv", None), P("rcv", "slab", None, None)),
        check_vma=False,
    )
```

```python
import functools

import jax
import jax.numpy as jnp
from jax import lax
from jax.experimental import pallas as pl
from jax.experimental.pallas import tpu as pltpu
from jax.sharding import PartitionSpec as P

MESH = pl.DeviceIdType.MESH
F32 = jnp.float32
SNAPS = 4
STEPS = 8
CORES = 2
ZHI = 4
ZLO = 4
ROWS = 4
CHUNKS = 8
PAD = 8
PARCELS = ((0, 4), (4, 7), (7, 8))
A, B, M = 0, 1, 2


def when(condition, action):
    pl.when(condition)(action)


def kernel(
    dims,
    now_ref,
    before_ref,
    courant_ref,
    log_ref,
    store_ref,
    owner_ref,
    cell_ref,
    trace_ref,
    weight_ref,
    sens_ref,
    after_ref,
    field,
    log_buf,
    courant,
    grad,
    weighted,
    group_in,
    snap_in,
    parcel_out,
    snap_tile,
    sum_tile,
    load_sem,
    model_send,
    model_recv,
    halo_send,
    halo_recv,
    group_send,
    group_recv,
    snap_send,
    snap_recv,
    parcel_send,
    parcel_recv,
    out_sem,
    relay,
):
    slabs, xs, ny, nz = dims
    group = xs * CORES
    block = ny // group
    pairs = ZHI // CORES
    chunk = ny // CHUNKS
    s = lax.axis_index("slab")
    r = lax.axis_index("rcv")
    core = lax.rem(r, CORES)
    zh = lax.rem(r // CORES, ZHI)
    xpos = r // (CORES * ZHI)
    member = xpos * CORES + core
    has_left, has_right = s > 0, s < slabs - 1

    def rcv_of(x, z, c):
        return (x * ZHI + z) * CORES + c

    def peer(d):
        other = lax.rem(member + d, group)
        return rcv_of(other // CORES, zh, lax.rem(other, CORES))

    barrier = pltpu.get_barrier_semaphore()

    def greet(slab, rcv):
        pl.semaphore_signal(barrier, 1, device_id=(slab, rcv), device_id_type=MESH)

    when(has_left, lambda: greet(s - 1, r))
    when(has_right, lambda: greet(s + 1, r))
    for d in range(1, group):
        greet(s, peer(d))
    half = zh // pairs

    columns = slabs // ZLO
    zline = zh * ZLO + s // columns
    length = ZHI * ZLO

    def along(d, c=core):
        z = lax.rem(zline + d + length, length)
        return lax.rem(z, ZLO) * columns + lax.rem(s, columns), rcv_of(xpos, z // ZLO, c)

    for d in (-1, 1):
        for c in range(CORES):
            greet(*along(d, c))

    def relay_signal(n):
        for d in (-(2**n), 2**n):
            pl.semaphore_signal(relay.at[n], 1, device_id=along(d), device_id_type=MESH)

    def relay_wait(n):
        pl.semaphore_wait(relay.at[n], 2)

    own = pl.ds(ROWS, ROWS)
    ycells = pl.ds(PAD, ny)
    loads = [
        pltpu.make_async_copy(log_ref, log_buf.at[own, ycells], load_sem.at[0]),
        pltpu.make_async_copy(courant_ref, courant.at[own], load_sem.at[1]),
        pltpu.make_async_copy(now_ref.at[0], field.at[A, own, ycells], load_sem.at[2]),
        pltpu.make_async_copy(before_ref.at[0], field.at[M, own, ycells], load_sem.at[3]),
        pltpu.make_async_copy(
            store_ref.at[0, :, pl.ds(pl.multiple_of(member * block, 8), block)],
            snap_in.at[group - 1],
            load_sem.at[4],
        ),
    ]
    for load in loads:
        load.start()

    zero_pad = jnp.zeros((3 * ROWS, PAD, nz), F32)
    for slot in (A, B, M):
        field[slot, :, 0:PAD, :] = zero_pad
        field[slot, :, PAD + ny : 2 * PAD + ny, :] = zero_pad
    log_buf[:, 0:PAD, :] = zero_pad
    log_buf[:, PAD + ny : 2 * PAD + ny, :] = zero_pad

    def clear(lo):
        def body(i, carry):
            rows = pl.ds(pl.multiple_of(i * 8, 8), 8)
            shifted = pl.ds(pl.multiple_of(i * 8 + PAD, 8), 8)
            zeros = jnp.zeros((8, nz), F32)
            for row in range(lo, lo + ROWS):
                for slot in (A, B, M):
                    field[slot, row, shifted, :] = zeros
                log_buf[row, shifted, :] = zeros
                courant[row, rows, :] = zeros
            return carry

        lax.fori_loop(0, ny // 8, body, 0)

    when(jnp.logical_not(has_left), lambda: clear(0))
    when(jnp.logical_not(has_right), lambda: clear(2 * ROWS))

    neighbours = has_left.astype(jnp.int32) + has_right.astype(jnp.int32)
    pl.semaphore_wait(barrier, neighbours + (group - 1) + 2 * CORES)

    def side_copy(side, src, dst, send, recv):
        return pltpu.make_async_remote_copy(
            src_ref=src,
            dst_ref=dst,
            send_sem=send,
            recv_sem=recv,
            device_id=(s + 1 if side == 0 else s - 1, r),
            device_id_type=MESH,
        )

    leaves = (has_right, has_left)
    comes = (has_left, has_right)

    def model_copy(which, side):
        near = (2, 0)[side]
        far = (0, 2)[side]
        land_near = (2, 8)[side]
        land_far = (0, 10)[side]
        part = pl.ds(pl.multiple_of(core * (ny // 2), 8), ny // 2)
        shifted = pl.ds(pl.multiple_of(core * (ny // 2) + PAD, 8), ny // 2)
        if which == 2:
            src, dst = courant_ref.at[near : near + 2, part], courant.at[land_near : land_near + 2, part]
        else:
            at, to = ((near, land_near), (far, land_far))[which]
            src, dst = log_ref.at[at : at + 2, part], log_buf.at[to : to + 2, shifted]
        return side_copy(side, src, dst, model_send.at[which, side], model_recv.at[which, side])

    def share_copy(which, side):
        part = pl.ds(pl.multiple_of(core * (ny // 2), 8), ny // 2)
        shifted = pl.ds(pl.multiple_of(core * (ny // 2) + PAD, 8), ny // 2)
        if which == 2:
            at = (2, 8)[side]
            block_ref = courant.at[at : at + 2, part]
        else:
            at = ((2, 8), (0, 10))[which][side]
            block_ref = log_buf.at[at : at + 2, shifted]
        return pltpu.make_async_remote_copy(
            src_ref=block_ref,
            dst_ref=block_ref,
            send_sem=model_send.at[which + 3, side],
            recv_sem=model_recv.at[which + 3, side],
            device_id=(s, rcv_of(xpos, zh, 1 - core)),
            device_id_type=MESH,
        )

    def share_start(which):
        for side in (0, 1):
            when(comes[side], model_copy(which, side).wait_recv)
            when(comes[side], share_copy(which, side).start)

    def share_wait(which):
        for side in (0, 1):
            when(comes[side], share_copy(which, side).wait)

    def halo_copy(e, side, j, deep, slot, from_input=False):
        if deep == ROWS:
            at, to = 0, (0, 2 * ROWS)[side]
        else:
            at, to = (ROWS - deep, 0)[side], (ROWS - deep, 2 * ROWS)[side]
        here = pl.ds(pl.multiple_of(j * chunk, 8), chunk)
        there = pl.ds(pl.multiple_of(j * chunk + PAD, 8), chunk)
        if from_input:
            src = now_ref.at[0, at : at + deep, here]
        else:
            src = field.at[slot, ROWS + at : ROWS + at + deep, there]
        dst = field.at[slot, to : to + deep, there]
        return side_copy(side, src, dst, halo_send.at[e, side, j], halo_recv.at[e, side, j])

    def halo_start(e, j, deep, slot, from_input=False):
        for side in (0, 1):
            copy = halo_copy(e, side, j, deep, slot, from_input)
            when(leaves[side], copy.start)

    def halo_arrive(e, j, deep, slot):
        for side in (0, 1):
            copy = halo_copy(e, side, j, deep, slot)
            when(comes[side], copy.wait_recv)

    def halo_sent(e, deep, slot, from_input=False):
        def body(j, carry):
            for side in (0, 1):
                copy = halo_copy(e, side, j, deep, slot, from_input)
                when(leaves[side], copy.wait_send)
            return carry

        lax.fori_loop(0, CHUNKS, body, 0)

    for side in (0, 1):
        when(leaves[side], model_copy(0, side).start)
    for j in range(CHUNKS):
        halo_start(0, j, 2, A, True)
    for which in (1, 2):
        for side in (0, 1):
            when(leaves[side], model_copy(which, side).start)
    relay_signal(0)

    def snap_copy(d):
        other = lax.rem(member + d, group)
        return pltpu.make_async_remote_copy(
            src_ref=store_ref.at[0, :, pl.ds(pl.multiple_of(other * block, 8), block)],
            dst_ref=snap_in.at[d - 1],
            send_sem=snap_send.at[d - 1],
            recv_sem=snap_recv.at[d - 1],
            device_id=(s, peer(d)),
            device_id_type=MESH,
        )

    lane = lax.broadcasted_iota(jnp.int32, (8, nz), 1)
    ids = lax.broadcasted_iota(jnp.int32, (8, nz), 0) * nz + lane
    low1, low2 = lane >= 1, lane >= 2
    high1, high2 = lane < nz - 1, lane < nz - 2

    def z_shifts(u):
        zero = jnp.zeros_like(u)
        return (
            jnp.where(low2, pltpu.roll(u, 2, 1), zero),
            jnp.where(low1, pltpu.roll(u, 1, 1), zero),
            jnp.where(high1, pltpu.roll(u, nz - 1, 1), zero),
            jnp.where(high2, pltpu.roll(u, nz - 2, 1), zero),
        )

    twelfth = 1.0 / 12.0

    def slopes(rows):
        def body(i, carry):
            at = pl.ds(pl.multiple_of(i * 8, 8), 8)
            y0 = i * 8 + PAD
            mid = {}
            for row in rows:
                for k in (-2, -1, 0, 1, 2):
                    if row + k not in mid:
                        mid[row + k] = log_buf[row + k, pl.ds(pl.multiple_of(y0, 8), 8), :]
            results = []
            for row in rows:
                y = [log_buf[row, pl.ds(y0 + k, 8), :] for k in (-2, -1, 1, 2)]
                z = z_shifts(mid[row])
                x = [mid[row + k] for k in (-2, -1, 1, 2)]
                for axis, u in enumerate((x, y, z)):
                    slope = (8.0 * (u[2] - u[1]) - (u[3] - u[0])) * twelfth
                    results.append((axis, row, slope))
            scaled = [(row, courant[row, at, :] * twelfth) for row in rows]
            for axis, row, slope in results:
                grad[axis, row, at, :] = slope
            for row, value in scaled:
                courant[row, at, :] = value
            return carry

        lax.fori_loop(0, ny // 8, body, 0)

    cell = cell_ref[0]
    weight = weight_ref[0]

    def advance(dst, src, prev, rows, start, amplitude, snap=None, blocks=2):
        results = []
        for offset in range(blocks):
            i = start + offset
            at = pl.ds(pl.multiple_of(i * 8, 8), 8)
            y0 = i * 8 + PAD
            centre = pl.ds(pl.multiple_of(y0, 8), 8)
            mid = {row: field[src, row, centre, :] for row in range(rows[0] - 2, rows[-1] + 3)}
            for row in rows:
                u = mid[row]
                y = [field[src, row, pl.ds(y0 + k, 8), :] for k in (-2, -1, 1, 2)]
                z = z_shifts(u)
                x = [mid[row + k] for k in (-2, -1, 1, 2)]
                near = (x[1] + x[2]) + (y[1] + y[2]) + (z[1] + z[2])
                far = (x[0] + x[3]) + (y[0] + y[3]) + (z[0] + z[3])
                drift = [
                    grad[axis, row, at, :] * (8.0 * (v[2] - v[1]) - (v[3] - v[0]))
                    for axis, v in enumerate((x, y, z))
                ]
                change = (16.0 * near - far - 90.0 * u) + (drift[0] + drift[1] + drift[2])
                new = (2.0 * u - field[prev, row, centre, :]) + courant[row, at, :] * change
                base = ((s * ROWS + (row - ROWS)) * ny + i * 8) * nz
                new = new + jnp.where(ids == cell - base, amplitude, 0.0)
                results.append((row, at, centre, new))
        for row, at, centre, new in results:
            field[dst, row, centre, :] = new
            if snap is not None:
                weighted[snap, row - ROWS, at, :] = weight * new

    own_rows = range(ROWS, 2 * ROWS)
    wide_rows = range(ROWS - 2, 2 * ROWS + 2)
    per = chunk // 16

    def group_copy(k, other):
        d = lax.rem(other - member + group, group)
        return d, pltpu.make_async_remote_copy(
            src_ref=weighted.at[k, :, pl.ds(pl.multiple_of(other * block, 8), block)],
            dst_ref=group_in.at[k, jnp.maximum(d - 1, 0)],
            send_sem=group_send.at[k, jnp.maximum(d - 1, 0)],
            recv_sem=group_recv.at[k, jnp.maximum(d - 1, 0)],
            device_id=(s, rcv_of(other // CORES, zh, lax.rem(other, CORES))),
            device_id_type=MESH,
        )

    def group_start(k, j):
        for other in range(group // CHUNKS):
            d, copy = group_copy(k, j * (group // CHUNKS) + other)
            when(d > 0, copy.start)

    def group_wait(k, arrival):
        for d in range(1, group):
            copy = group_copy(k, lax.rem(member + d, group))[1]
            if arrival:
                copy.wait_recv()
            else:
                copy.wait_send()

    pieces = [(i, c, (2 * i + c) * 4) for i in range(pairs) for c in range(CORES)]

    def landing(part, z):
        lo, hi = PARCELS[part]
        return snap_tile.at[z] if part == 0 else sum_tile.at[z, lo - SNAPS : hi - SNAPS]

    def parcel_copy(part, i, c):
        lo, hi = PARCELS[part]
        z = core * pairs + i
        return (z == zh) & (c == core), pltpu.make_async_remote_copy(
            src_ref=parcel_out.at[i, c, lo:hi],
            dst_ref=landing(part, zh),
            send_sem=parcel_send.at[part, i, c],
            recv_sem=parcel_recv.at[part, zh],
            device_id=(s, rcv_of(xpos, z, c)),
            device_id_type=MESH,
        )

    def parcel_start(part):
        lo, hi = PARCELS[part]
        for i, c, at in pieces:
            to_self, copy = parcel_copy(part, i, c)
            when(jnp.logical_not(to_self), copy.start)

            @pl.when(to_self)
            def _():
                for n in range(lo, hi):
                    landing(part, zh)[n - lo] = parcel_out[i, c, n]

    def parcel_sent(part):
        for i, c, at in pieces:
            to_self, copy = parcel_copy(part, i, c)
            when(jnp.logical_not(to_self), copy.wait_send)

    def parcel_arrive(part):
        for z in range(ZHI):
            copy = pltpu.make_async_remote_copy(
                src_ref=landing(part, z),
                dst_ref=landing(part, z),
                send_sem=parcel_recv.at[part, z],
                recv_sem=parcel_recv.at[part, z],
                device_id=(s, rcv_of(xpos, z, half)),
                device_id_type=MESH,
            )
            when((z != zh) | (half != core), copy.wait_recv)

    def sum_tiles(k):
        group_wait(k, True)
        results = []
        for i, c, at in pieces:
            for row in range(ROWS):
                terms = [weighted[k, row, pl.ds(member * block + at, 4), :]]
                terms += [group_in[k, d, row, at : at + 4, :] for d in range(group - 1)]
                while len(terms) > 1:
                    terms = [a + b for a, b in zip(terms[::2], terms[1::2])]
                results.append((i, c, row, terms[0]))
        for i, c, row, total in results:
            parcel_out[i, c, SNAPS + k, row] = total

    def snap_tiles():
        loads[4].wait()
        for d in range(1, group):
            snap_copy(d).wait_recv()
        for k in range(SNAPS):
            slot = owner_ref[k]
            holder = (slot // (CORES * ZHI)) * CORES + lax.rem(slot, CORES)
            place = lax.rem(member - holder + 2 * group - 1, group)
            results = [
                (i, c, row, snap_in[place, row, at : at + 4, :])
                for i, c, at in pieces
                for row in range(ROWS)
            ]
            for i, c, row, value in results:
                parcel_out[i, c, k, row] = value

    loads[0].wait()
    loads[1].wait()
    share_start(0)
    share_wait(0)
    slopes(own_rows)
    loads[2].wait()
    loads[3].wait()
    relay_wait(0)
    relay_signal(1)

    def first(j, carry):
        halo_arrive(0, j, 2, A)

        def body(i, inner):
            advance(M, A, M, own_rows, 2 * i, trace_ref[0, 0])
            return inner

        lax.fori_loop(j * per, (j + 1) * per, body, 0)
        halo_start(1, j, 2, M)
        return carry

    lax.fori_loop(0, CHUNKS, first, 0)
    for d in range(1, group):
        snap_copy(d).start()
    for which in (1, 2):
        share_start(which)
    relay_wait(1)
    relay_signal(2)

    def second(j, carry):
        halo_arrive(1, j, 2, M)

        def body(i, inner):
            advance(B, M, A, own_rows, 2 * i, trace_ref[0, 1], 0)
            return inner

        lax.fori_loop(j * per, (j + 1) * per, body, 0)
        halo_start(2, j, ROWS, B)
        group_start(0, j)
        return carry

    lax.fori_loop(0, CHUNKS, second, 0)
    for which in (1, 2):
        share_wait(which)
    slopes((2, 3, 8, 9))
    relay_wait(2)
    halo_sent(0, 2, A, True)
    halo_sent(1, 2, M)

    def pair(p, carry):
        src = lax.rem(p, 2)
        dst = 1 - src

        @pl.when(p > 1)
        def _():
            halo_sent(p, ROWS, dst)

        def part(j, inner):
            @pl.when((p == 1) & (j == CHUNKS - 2))
            def _():
                snap_tiles()
                parcel_start(0)

            @pl.when((p == SNAPS - 1) & (j == 0))
            def _():
                for k in range(SNAPS - 2):
                    sum_tiles(k)

            @pl.when(j == 0)
            def _():
                halo_arrive(p + 1, 0, ROWS, src)

            @pl.when(j < CHUNKS - 1)
            def _():
                halo_arrive(p + 1, j + 1, ROWS, src)

            def middle(start, blocks):
                advance(M, src, M, wide_rows, start, trace_ref[0, 2 * p], None, blocks)

            when(j == 0, lambda: middle(0, 1))

            def ahead(i, deep):
                when(i < ny // 16 - 1, lambda: middle(2 * i + 1, 2))
                when(i == ny // 16 - 1, lambda: middle(2 * i + 1, 1))
                return deep

            lax.fori_loop(j * per, (j + 1) * per, ahead, 0)

            def final(i, deep):
                advance(dst, M, src, own_rows, 2 * i, trace_ref[0, 2 * p + 1], p)
                return deep

            lax.fori_loop(j * per, (j + 1) * per, final, 0)
            when(p < SNAPS - 1, lambda: halo_start(p + 2, j, ROWS, dst))
            group_start(p, j)

            @pl.when((p == SNAPS - 1) & (j == CHUNKS - 2))
            def _():
                sum_tiles(SNAPS - 2)
                parcel_start(1)

            @pl.when(p == SNAPS - 1)
            def _():
                at = pl.ds(pl.multiple_of(j * chunk, 8), chunk)
                there = pl.ds(pl.multiple_of(j * chunk + PAD, 8), chunk)
                pltpu.make_async_copy(
                    field.at[dst, own, there], after_ref.at[0, :, at], out_sem.at[j]
                ).start()

            return inner

        lax.fori_loop(0, CHUNKS, part, 0)
        return carry

    lax.fori_loop(1, SNAPS, pair, 0)
    sum_tiles(SNAPS - 1)
    parcel_start(2)

    halo_sent(SNAPS, ROWS, B)
    for which in range(3):
        for side in (0, 1):
            when(leaves[side], model_copy(which, side).wait_send)
    for d in range(1, group):
        snap_copy(d).wait_send()
    for k in range(SNAPS):
        group_wait(k, False)
    for j in range(CHUNKS):
        at = pl.ds(j * chunk, chunk)
        there = pl.ds(j * chunk + PAD, chunk)
        pltpu.make_async_copy(field.at[A, own, there], after_ref.at[0, :, at], out_sem.at[j]).wait()

    def kernel_term(k):
        total = (sum_tile[0, k] + sum_tile[1, k]) + (sum_tile[2, k] + sum_tile[3, k])
        holder = lax.rem(owner_ref[k] // CORES, ZHI)
        return total * snap_tile[holder, k]

    parcel_sent(0)
    parcel_sent(1)
    parcel_arrive(0)
    parcel_arrive(1)
    early = (kernel_term(0) + kernel_term(1)) + kernel_term(2)
    parcel_arrive(2)
    sens_ref[...] = early + kernel_term(SNAPS - 1)
    parcel_sent(2)


def local(mesh, now, before, courant, log, store, owner, cells, traces, weights):
    rows, ny, nz = courant.shape
    slabs, receivers = mesh.shape["slab"], mesh.shape["rcv"]
    xs = receivers // (ZHI * CORES)
    group = xs * CORES
    block = ny // group
    pairs = ZHI // CORES
    any_space = pl.BlockSpec(memory_space=pltpu.HBM)
    scalar = pl.BlockSpec(memory_space=pltpu.SMEM)
    dma = pltpu.SemaphoreType.DMA
    tall = ny + 2 * PAD
    return pl.pallas_call(
        functools.partial(kernel, (slabs, xs, ny, nz)),
        out_shape=(
            jax.ShapeDtypeStruct((rows, ny // receivers, nz), F32),
            jax.ShapeDtypeStruct(now.shape, F32),
        ),
        in_specs=[any_space] * 5 + [scalar] * 4,
        out_specs=(pl.BlockSpec(memory_space=pltpu.VMEM), any_space),
        scratch_shapes=[
            pltpu.VMEM((3, 3 * ROWS, tall, nz), F32),
            pltpu.VMEM((3 * ROWS, tall, nz), F32),
            pltpu.VMEM((3 * ROWS, ny, nz), F32),
            pltpu.VMEM((3, 3 * ROWS, ny, nz), F32),
            pltpu.VMEM((SNAPS, ROWS, ny, nz), F32),
            pltpu.VMEM((SNAPS, group - 1, ROWS, block, nz), F32),
            pltpu.VMEM((group, ROWS, block, nz), F32),
            pltpu.VMEM((pairs, CORES, 2 * SNAPS, ROWS, 4, nz), F32),
            pltpu.VMEM((ZHI, SNAPS, ROWS, 4, nz), F32),
            pltpu.VMEM((ZHI, SNAPS, ROWS, 4, nz), F32),
            dma((5,)),
            dma((6, 2)),
            dma((6, 2)),
            dma((SNAPS + 1, 2, CHUNKS)),
            dma((SNAPS + 1, 2, CHUNKS)),
            dma((SNAPS, group - 1)),
            dma((SNAPS, group - 1)),
            dma((group - 1,)),
            dma((group - 1,)),
            dma((len(PARCELS), pairs, CORES)),
            dma((len(PARCELS), ZHI)),
            dma((CHUNKS,)),
            pltpu.SemaphoreType.REGULAR((3,)),
        ],
        compiler_params=pltpu.CompilerParams(
            collective_id=0, has_side_effects=True, vmem_limit_bytes=60 * 1024 * 1024
        ),
        name="adjoint",
    )(now, before, courant, log, store, owner, cells, traces, weights)


def solution(mesh):
    placed = (
        P("rcv", "slab", None, None),
        P("rcv", "slab", None, None),
        P("slab", None, None),
        P("slab", None, None),
        P("rcv", "slab", None, None),
        P(),
        P("rcv"),
        P("rcv", None),
        P("rcv"),
    )
    return jax.shard_map(
        functools.partial(local, mesh),
        mesh=mesh,
        in_specs=placed,
        out_specs=(P("slab", "rcv", None), P("rcv", "slab", None, None)),
        check_vma=False,
    )
```
